256 devices in a mesh: attn: 16 (over z, core), ffn: 8 (over x, y_hi), grp: 2 (over y_lo).
Axes of the slice: x: 4, y: 4 (y_hi: 2, y_lo: 2; y = y_hi * 2 + y_lo), z: 8, core: 2. Of those that a mesh axis runs over, the one named last changes fastest.
Arguments:
- resid: bfloat16 [256, 12288], P('attn', ('ffn', 'grp')), may hold values from -6 to 6
- query: bfloat16 [256, 12288], P('attn', ('ffn', 'grp')), may hold values from -2.5 to 2.5
- key_new: bfloat16 [256, 12288], P('attn', ('ffn', 'grp')), may hold values from -2.5 to 2.5
- value_new: bfloat16 [256, 12288], P('attn', ('ffn', 'grp')), may hold values from -6 to 6
- key_cache: bfloat16 [256, 128, 12288], P('attn', None, ('ffn', 'grp')), may hold values from -2.5 to 2.5
- value_cache: bfloat16 [256, 128, 12288], P('attn', None, ('ffn', 'grp')), may hold values from -6 to 6
- lengths: int32 [256], P('attn'), may hold values from 1 to 128, as said below
- norm_gain: float32 [12288], replicated, may hold values from 0.5 to 1.5
- active: int32 [64, 64], replicated, may hold values from 0 to 255, all different within a row; in each aligned block of 4 rows (0 to 3, 4 to 7, ...) at most 2 rows name the same one
- up_weight: bfloat16 [12288, 32768], P(None, ('attn', 'ffn', 'grp')), may hold values from -0.0546875 to 0.0546875
- down_weight: bfloat16 [32768, 12288], P(('attn', 'ffn', 'grp')), may hold values from -0.0625 to 0.0625
Outputs:
- layer_out: bfloat16 [256, 12288], P('attn', ('ffn', 'grp'))
The draws below stay inside these ranges and needn't reach their ends.
Inputs may be any that keep to these rules, and one draw needn't show every extreme that they name: `lengths`: some request has exactly 128 entries. `active`: each row names 64 different blocks; among the 4 row blocks of one attention index (rows a * 4 to a * 4 + 3) at most 2 name the same block, and some block is named by exactly 2 of them.
All inputs are finite; a program needn't handle non-finite values.
Results may differ from the reference program's by a relative error of at most 0.015.
Values may be sent and summed in bfloat16 or wider, within the bound.
A program may use at most 128 MiB of HBM per device.

```python
import math
import jax
import jax.numpy as jnp
import numpy as np
from jax import lax

H = 96
HD = 128
D = 12288
BLOCK = 128
BLOCKS = 256
FF = 32768
R_DEV = 16
REQ = 256
MAXLEN = 128
NCH = 4
RCH = 4
NCHUNK = 64
ACT = 64
SLOT = 2


def draw_lengths(key, part):
    key = jax.random.fold_in(key, 11)
    key_caps, key_draw, key_spot = jax.random.split(key, 3)
    groups = REQ // R_DEV
    cap_rows = jax.random.randint(key_caps, (groups, 1), MAXLEN // 4 + 1, MAXLEN + 1)
    raw_draw = jax.random.randint(key_draw, (groups, R_DEV), 0, 1 << 20)
    length_rows = (raw_draw % cap_rows + 1).reshape(REQ)
    spot_index = jax.random.randint(key_spot, (), 0, REQ)
    return length_rows.at[spot_index].set(MAXLEN).astype(jnp.int32)


def block_scale(rng, dims, cuts, low, high):
    loudness, own = 1.0, jax.random.fold_in(rng, 6)
    for axis_at, blocks in cuts:
        steps = jnp.exp(jax.random.uniform(jax.random.fold_in(own, axis_at), (blocks,), jnp.float32, low / len(cuts), high / len(cuts)))
        loudness = loudness * jnp.repeat(steps, dims[axis_at] // blocks).reshape([-1 if axis == axis_at else 1 for axis in range(len(dims))])
    return loudness


def shared_out(rng, own, number, rows, count, top, reach, slope):
    ranking = jax.random.permutation(rng, count)
    crowded, usual = portions_of(count, rows * top, reach, slope, True), portions_of(count, rows * top, reach, slope, False)
    places = jnp.arange(count)

    def named(sizes, offset_by):
        used = int((sizes > 0).sum())
        fixed = max(1, used // 4)
        moved = fixed + (places - fixed + offset_by * (used - fixed)) % max(1, count - fixed)
        return jnp.zeros((count,), jnp.int32).at[ranking[jnp.where(places < fixed, places, moved)]].set(jnp.asarray(sizes, jnp.int32))

    sizes = jnp.where(number % 4 == 0, named(crowded, number // 4), named(usual, number - number // 4 - 1))
    mixed = jax.random.permutation(jax.random.fold_in(own, 3), count)
    giver, sink = mixed[0:count // 2 * 2:2], mixed[1:count // 2 * 2:2]
    room = jnp.minimum(sizes[giver] - 1, reach - sizes[sink]) // 2
    room = jnp.where((giver == ranking[0]) | (sink == ranking[0]) | (sizes[sink] == 0), 0, jnp.maximum(room, 0))
    moved = jax.random.randint(jax.random.fold_in(own, 4), (count // 2,), 0, 1 << 20) % (room + 1)
    sizes = sizes.at[giver].add(-moved).at[sink].add(moved)
    members = jnp.searchsorted(jnp.cumsum(sizes), jnp.arange(rows * top), side="right").astype(jnp.int32)
    table = members.reshape(top, rows).T
    table = table[jax.random.permutation(jax.random.fold_in(own, 1), rows)]
    offset_by = jax.random.randint(jax.random.fold_in(own, 2), (rows, 1), 0, top)
    return jnp.take_along_axis(table, (jnp.arange(top)[None, :] + offset_by) % top, axis=1)


def portions_of(count, total, reach, lean, full):
    loads = [(1 << 20) // math.isqrt(rank ** lean) + 1 for rank in range(1, count + 1)]
    largest = reach if full else min(reach, max(-(-total // count), total * loads[0] // sum(loads)))
    least = 1 if total - largest >= count - 1 else 0
    counts, rest = [largest] + [least] * (count - 1), total - largest - least * (count - 1)
    while rest > 0:
        free = [i for i in range(1, count) if counts[i] < largest] or [i for i in range(1, count) if counts[i] < reach]
        pool, left = sum([loads[i] for i in free]), rest
        for i in free:
            more = min(reach - counts[i], max(1, left * loads[i] // pool), rest)
            counts[i] = counts[i] + more
            rest = rest - more
    return np.array(counts)


def normal_values(own_key, extent, spread, bound, shards=(), kind=jnp.bfloat16):
    result = spread * jax.random.normal(own_key, extent, jnp.float32)
    if shards:
        result = result * block_scale(own_key, extent, shards, -0.22, 0.18)
    return jnp.clip(result, -bound, bound).astype(kind)


def setup_inputs(seed: int = 0) -> dict:
    arg_keys = jax.random.split(jax.random.key(seed), 12)
    resid = normal_values(arg_keys[0], (REQ, D), 1.0, 6.0, ((0, 16), (1, 16)))
    query = normal_values(arg_keys[1], (REQ, D), 1.0, 2.5, ((0, 16), (1, 16)))
    key_new = normal_values(arg_keys[2], (REQ, D), 1.0, 2.5, ((0, 16), (1, 16)))
    value_new = normal_values(arg_keys[3], (REQ, D), 1.0, 6.0, ((0, 16), (1, 16)))
    key_cache = normal_values(arg_keys[4], (REQ, MAXLEN, D), 1.0, 2.5, ((0, 16), (2, 16)))
    value_cache = normal_values(arg_keys[5], (REQ, MAXLEN, D), 1.0, 6.0, ((0, 16), (2, 16)))
    lengths = draw_lengths(jax.random.fold_in(arg_keys[11], 71), 0)
    norm_gain = jnp.clip(1.0 + 0.1 * jax.random.normal(arg_keys[7], (D,), jnp.float32), 0.5, 1.5)
    active_keys = jax.random.split(jax.random.fold_in(arg_keys[8], 1), NCHUNK // NCH)
    active_turns = jax.random.permutation(jax.random.fold_in(arg_keys[8], 3), NCHUNK // NCH)
    active = jax.vmap(lambda own, number: shared_out(jax.random.fold_in(arg_keys[8], 2), own, number, NCH, BLOCKS, ACT, SLOT, 2))(active_keys, active_turns).reshape((NCHUNK, ACT))
    up_weight = normal_values(arg_keys[9], (D, FF), D ** -0.5, 0.0546875, ((1, 256),))
    down_weight = normal_values(arg_keys[10], (FF, D), (ACT * BLOCK) ** -0.5, 0.0625, ((0, 256),))
    return dict(resid=resid, query=query, key_new=key_new, value_new=value_new, key_cache=key_cache, value_cache=value_cache, lengths=lengths, norm_gain=norm_gain, active=active, up_weight=up_weight, down_weight=down_weight)


def attend_one(query_row, key_rows, value_rows, key_own, value_own, length):
    scale = HD ** (-0.5)
    query_heads = query_row.astype(jnp.float32).reshape(H, HD)
    key_heads = key_rows.astype(jnp.float32).reshape(MAXLEN, H, HD)
    value_heads = value_rows.astype(jnp.float32).reshape(MAXLEN, H, HD)
    scores = jnp.einsum('hd,jhd->hj', query_heads, key_heads) * scale
    own_score = lax.optimization_barrier(jnp.sum(query_heads * key_own.astype(jnp.float32).reshape(H, HD), axis=-1)) * scale
    positions = jnp.arange(MAXLEN, dtype=jnp.int32)
    expo = jnp.where(positions[None, :] < length, jnp.exp(scores), jnp.float32(0.0))
    own_exp = jnp.exp(own_score)
    denom = lax.optimization_barrier(jnp.sum(expo, axis=-1)) + own_exp
    weights = (expo / denom[:, None]).astype(jnp.bfloat16)
    own_weight = (own_exp / denom).astype(jnp.bfloat16)
    mixed = jnp.einsum('hj,jhd->hd', weights.astype(jnp.float32), value_heads)
    mixed = mixed + own_weight.astype(jnp.float32)[:, None] * value_own.astype(jnp.float32).reshape(H, HD)
    return mixed.reshape(H * HD)

def reference(resid, query, key_new, value_new, key_cache, value_cache, lengths, norm_gain, active, up_weight, down_weight):

    def attend_packed(packed):
        return attend_one(*packed)
    attended = lax.map(attend_packed, (query, key_cache, value_cache, key_new, value_new, lengths))
    stream = (resid.astype(jnp.float32) + attended).astype(jnp.bfloat16)
    values = stream.astype(jnp.float32)
    mean_row = lax.optimization_barrier(jnp.mean(values, axis=1, keepdims=True))
    centred = values - mean_row
    var_row = lax.optimization_barrier(jnp.mean(centred * centred, axis=1, keepdims=True))
    normed = (centred * lax.rsqrt(var_row + 1e-05) * norm_gain[None, :]).astype(jnp.bfloat16)
    block_hits = jnp.any(active[:, :, None] == jnp.arange(BLOCKS, dtype=jnp.int32)[None, None, :], axis=1)
    row_hits = jnp.repeat(block_hits.astype(jnp.float32), RCH, axis=0)

    def add_block(total, index):
        first_col = (index * BLOCK).astype(jnp.int32)
        up_cols = lax.dynamic_slice_in_dim(up_weight, first_col, BLOCK, 1)
        down_rows = lax.dynamic_slice_in_dim(down_weight, first_col, BLOCK, 0)
        before = jnp.dot(normed, up_cols, preferred_element_type=jnp.float32)
        row_mask = lax.dynamic_slice_in_dim(row_hits, index.astype(jnp.int32), 1, 1)
        hidden = (jnp.maximum(before, 0.0) * row_mask).astype(jnp.bfloat16)
        return (total + jnp.dot(hidden, down_rows, preferred_element_type=jnp.float32), None)
    start_total = jnp.zeros((REQ, H * HD), jnp.float32)
    ffn, _ = lax.scan(add_block, start_total, jnp.arange(BLOCKS, dtype=jnp.int32))
    return (stream.astype(jnp.float32) + ffn).astype(jnp.bfloat16)
```

```python
import functools

import jax
import jax.numpy as jnp
from jax import lax
from jax.experimental import pallas as pl
from jax.experimental.pallas import tpu as pltpu
from jax.sharding import PartitionSpec as P

MESH = pl.DeviceIdType.MESH
HD = 128
BF = jnp.bfloat16
F32 = jnp.float32
NT = (((1,), (1,)), ((), ()))
R = 16
NZ = 8
ROWS = R * NZ
HALF = ROWS // 2
STEP = 4


def attend_kernel(len_ref, resid_ref, q_ref, kn_ref, vn_ref, k_ref, v_ref, out_ref, qf, knf, vnf, att):
    at = pl.program_id(0)
    cols = resid_ref.shape[1]
    scale = HD ** (-0.5)

    @pl.when(at == 0)
    def _():
        qf[...] = q_ref[...].astype(F32)
        knf[...] = kn_ref[...].astype(F32)
        vnf[...] = vn_ref[...].astype(F32)

    head_of = lax.broadcasted_iota(jnp.int32, (8, cols), 1) // HD
    mine = head_of == lax.broadcasted_iota(jnp.int32, (8, cols), 0)
    place = lax.broadcasted_iota(jnp.int32, (8, HD), 1)
    for t in range(STEP):
        r = at * STEP + t
        heads = jnp.where(mine, qf[pl.ds(r, 1), :], 0.0)
        scores = lax.dot_general(heads.astype(BF), k_ref[t], NT, preferred_element_type=F32) * scale
        own = jnp.sum(heads * knf[pl.ds(r, 1), :], axis=1, keepdims=True) * scale
        expo = jnp.where(place < len_ref[r], jnp.exp(scores), 0.0)
        own_exp = jnp.exp(own)
        denom = jnp.sum(expo, axis=1, keepdims=True) + own_exp
        weights = (expo / denom).astype(BF)
        own_weight = (own_exp / denom).astype(BF).astype(F32)
        mixed = jnp.dot(weights, v_ref[t], preferred_element_type=F32) + own_weight * vnf[pl.ds(r, 1), :]
        att[pl.ds(r, 1), :] = jnp.sum(jnp.where(mine, mixed, 0.0), axis=0, keepdims=True)

    @pl.when(at == pl.num_programs(0) - 1)
    def _():
        out_ref[...] = (resid_ref[...].astype(F32) + att[...]).astype(BF)


def attend(resid, query, key_new, value_new, key_cache, value_cache, lengths):
    cols = resid.shape[1]
    whole = pl.BlockSpec((R, cols), lambda i: (0, 0))
    cache = pl.BlockSpec((STEP, 128, cols), lambda i: (i, 0, 0))
    return pl.pallas_call(
        attend_kernel,
        grid=(R // STEP,),
        out_shape=jax.ShapeDtypeStruct((R, cols), BF),
        in_specs=[pl.BlockSpec(memory_space=pltpu.SMEM), whole, whole, whole, whole, cache, cache],
        out_specs=whole,
        scratch_shapes=[pltpu.VMEM((R, cols), F32)] * 4,
        compiler_params=pltpu.CompilerParams(vmem_limit_bytes=32 * 1024 * 1024),
        name="attend",
    )(lengths, resid, query, key_new, value_new, key_cache, value_cache)


def ffn_kernel(
    stream_ref, gain_ref, active_ref, up_ref, down_ref, out_ref,
    xbuf, wu, wd, stats, rowsf,
    ya, yr, yl, ra, rl, rr, pa, pr, pleft, qa, ql, qr, tz, rz,
    w_loc, w_send, w_recv, st_send, st_recv, z_send, z_recv, p1_send, p1_recv, p2_send, p2_recv,
    a_send, a_recv, b_send, b_recv, c_send, c_recv, zz_send, zz_recv,
):
    attn, ffn, grp = lax.axis_index("attn"), lax.axis_index("ffn"), lax.axis_index("grp")
    z, core = attn // 2, attn % 2
    x, y = ffn // 2, (ffn % 2) * 2 + grp
    other = 1 - core
    p1 = x * other + y * core
    p2 = y * other + x * core
    cols = stream_ref.shape[1]
    width = 16 * cols

    def place(z_at, core_at, x_at, y_at):
        return (z_at * 2 + core_at, x_at * 2 + y_at // 2, y_at % 2)

    def near(i, j):
        q2, q1 = (p2 + i) % 4, (p1 + j) % 4
        return place(z, core, q1 * other + q2 * core, q2 * other + q1 * core)

    def group(i, j):
        q2, q1 = (p2 + i) % 4, (p1 + j) % 4
        return (q1 * other + q2 * core) * 4 + q2 * other + q1 * core

    def slot(i, j):
        return xbuf.at[(p2 + i) % 4, (p1 + j) % 4]

    def send(src, dst, s_sem, r_sem, device):
        copy = pltpu.make_async_remote_copy(
            src_ref=src, dst_ref=dst, send_sem=s_sem, recv_sem=r_sem, device_id=device, device_id_type=MESH
        )
        copy.start()
        started.append(copy)
        return copy

    def arrived(dst, r_sem):
        pltpu.make_async_remote_copy(
            src_ref=dst, dst_ref=dst, send_sem=r_sem, recv_sem=r_sem, device_id=near(0, 1), device_id_type=MESH
        ).wait_recv()

    started = []
    up_here = pltpu.make_async_copy(up_ref, wu.at[core], w_loc.at[0])
    up_here.start()
    down_rows = pl.ds(pl.multiple_of(core * 128, 128), 128)
    down_other = pl.ds(pl.multiple_of(other * 128, 128), 128)
    down_here = pltpu.make_async_copy(down_ref, wd.at[down_rows], w_loc.at[1])
    down_here.start()

    plane = [(i, j) for i in range(4) for j in range(4) if (i, j) != (0, 0)]
    barrier = pltpu.get_barrier_semaphore()
    partner = place(z, other, x, y)
    for i, j in plane:
        pl.semaphore_signal(barrier, inc=1, device_id=near(i, j), device_id_type=MESH)
    for k in range(1, NZ):
        pl.semaphore_signal(barrier, inc=1, device_id=place((z + k) % NZ, core, x, y), device_id_type=MESH)
    pl.semaphore_signal(barrier, inc=1, device_id=partner, device_id_type=MESH)
    pl.semaphore_wait(barrier, len(plane) + NZ)

    values = stream_ref[...].astype(F32)
    eye = (
        lax.broadcasted_iota(jnp.int32, (R, 128), 0) == lax.broadcasted_iota(jnp.int32, (R, 128), 1)
    ).astype(F32)
    own_mean = jnp.mean(values, axis=1, keepdims=True)
    off = values - own_mean
    own_sq = jnp.sum(off * off, axis=1, keepdims=True)
    here = stats.at[group(0, 0)]
    here[0:1, :] = jnp.sum(own_mean * eye, axis=0, keepdims=True)
    here[1:2, :] = jnp.sum(own_sq * eye, axis=0, keepdims=True)
    for n, (i, j) in enumerate(plane):
        send(here, here, st_send.at[n], st_recv.at[n], near(i, j))
    up_there = send(up_ref, wu.at[core], w_send.at[0], w_recv.at[0], partner)
    down_there = send(down_ref, wd.at[down_rows], w_send.at[1], w_recv.at[1], partner)
    for n, (i, j) in enumerate(plane):
        arrived(stats.at[group(4 - i, 4 - j)], st_recv.at[n])
    means, squares = stats[:, 0, :], stats[:, 1, :]
    mean_all = jnp.sum(means, axis=0, keepdims=True) * (1.0 / 16)
    gap = means - mean_all
    var_all = (jnp.sum(squares, axis=0, keepdims=True) + cols * jnp.sum(gap * gap, axis=0, keepdims=True)) * (
        1.0 / width
    )
    mean_row = jnp.sum(mean_all * eye, axis=1, keepdims=True)
    rstd_row = jnp.sum(lax.rsqrt(var_all + 1e-05) * eye, axis=1, keepdims=True)
    gain = gain_ref[pl.ds(group(0, 0), 1), :]
    z_rows = pl.ds(pl.multiple_of(z * R, R), R)
    mine = slot(0, 0)
    mine[z_rows, :] = ((values - mean_row) * rstd_row * gain).astype(BF)

    for k in range(1, NZ):
        send(mine.at[z_rows], mine.at[z_rows], z_send.at[k - 1], z_recv.at[k - 1], place((z + k) % NZ, core, x, y))

    block0 = z * 32 + group(0, 0)
    hit0 = jnp.max((active_ref[...] == block0).astype(F32), axis=1, keepdims=True)
    hit1 = jnp.max((active_ref[...] == block0 + 16).astype(F32), axis=1, keepdims=True)
    spans = active_ref.shape[0]
    hits = jnp.concatenate([jnp.broadcast_to(hit0, (spans, 128)), jnp.broadcast_to(hit1, (spans, 128))], axis=1)
    row_at = lax.broadcasted_iota(jnp.int32, (ROWS, spans), 0)
    span_at = lax.broadcasted_iota(jnp.int32, (ROWS, spans), 1)
    span_of = ((row_at // R) * 2 + core) * 4 + (row_at % R) // 4
    row_mask = jnp.dot((span_of == span_at).astype(BF), hits.astype(BF), preferred_element_type=F32)

    for k in range(1, NZ):
        from_rows = pl.ds(pl.multiple_of(((z + NZ - k) % NZ) * R, R), R)
        arrived(mine.at[from_rows], z_recv.at[k - 1])

    first, second = pl.ds(0, HALF), pl.ds(HALF, HALF)

    def spread(j):
        send(slot(0, j), slot(0, j), p2_send.at[0, j], p2_recv.at[0, j], near(1, 0))
        send(slot(0, j), slot(0, j), p2_send.at[1, j], p2_recv.at[1, j], near(3, 0))

    send(mine, mine, p1_send.at[0], p1_recv.at[0], near(0, 1))
    send(mine, mine, p1_send.at[1], p1_recv.at[1], near(0, 3))
    spread(0)
    up_here.wait()
    arrived(wu.at[other], w_recv.at[0])

    def up(i, j):
        rows = pl.ds(pl.multiple_of(group(i, j) * cols, 128), cols)
        both = jnp.concatenate([wu[0, rows, :], wu[1, rows, :]], axis=1)
        return jnp.dot(slot(i, j)[...], both, preferred_element_type=F32)

    before = up(0, 0)
    arrived(slot(0, 3), p1_recv.at[0])
    send(slot(0, 3).at[first], slot(0, 3).at[first], p1_send.at[2], p1_recv.at[2], near(0, 1))
    spread(3)
    arrived(slot(0, 1), p1_recv.at[1])
    send(slot(0, 1).at[second], slot(0, 1).at[second], p1_send.at[3], p1_recv.at[3], near(0, 3))
    spread(1)
    before += up(0, 3)
    before += up(0, 1)
    arrived(slot(0, 2).at[first], p1_recv.at[2])
    arrived(slot(0, 2).at[second], p1_recv.at[3])
    spread(2)
    before += up(0, 2)
    order = (0, 3, 1, 2)
    for j in order:
        arrived(slot(3, j), p2_recv.at[0, j])
        send(slot(3, j).at[first], slot(3, j).at[first], p2_send.at[2, j], p2_recv.at[2, j], near(1, 0))
        arrived(slot(1, j), p2_recv.at[1, j])
        send(slot(1, j).at[second], slot(1, j).at[second], p2_send.at[3, j], p2_recv.at[3, j], near(3, 0))
        before += up(3, j)
        before += up(1, j)
    for j in order:
        arrived(slot(2, j).at[first], p2_recv.at[2, j])
        arrived(slot(2, j).at[second], p2_recv.at[3, j])
        before += up(2, j)
    hidden = (jnp.maximum(before, 0.0) * row_mask).astype(BF)

    down_here.wait()
    arrived(wd.at[down_other], w_recv.at[1])

    def down(i, j):
        columns = pl.ds(pl.multiple_of(group(i, j) * cols, 128), cols)
        return jnp.dot(hidden, wd[:, columns], preferred_element_type=F32)

    back = (2, 3, 1, 0)
    for j in back:
        ya[j] = down(2, j).astype(BF)
        send(ya.at[j, first], ra.at[j, first], a_send.at[0, j], a_recv.at[0, j], near(1, 0))
        send(ya.at[j, second], ra.at[j, second], a_send.at[1, j], a_recv.at[1, j], near(3, 0))
    for j in back:
        part = down(1, j)
        yr[j, HALF:] = part[HALF:].astype(BF)
        arrived(ra.at[j, first], a_recv.at[0, j])
        yr[j, :HALF] = (part[:HALF] + ra[j, :HALF].astype(F32)).astype(BF)
        send(yr.at[j], rl.at[j], b_send.at[0, j], b_recv.at[0, j], near(1, 0))
        part = down(3, j)
        yl[j, :HALF] = part[:HALF].astype(BF)
        arrived(ra.at[j, second], a_recv.at[1, j])
        yl[j, HALF:] = (part[HALF:] + ra[j, HALF:].astype(F32)).astype(BF)
        send(yl.at[j], rr.at[j], b_send.at[1, j], b_recv.at[1, j], near(3, 0))

    def settled(j):
        part = down(0, j)
        arrived(rl.at[j], b_recv.at[0, j])
        part += rl[j].astype(F32)
        arrived(rr.at[j], b_recv.at[1, j])
        return part + rr[j].astype(F32)

    pa[...] = settled(2).astype(BF)
    send(pa.at[first], qa.at[first], c_send.at[0], c_recv.at[0], near(0, 1))
    send(pa.at[second], qa.at[second], c_send.at[1], c_recv.at[1], near(0, 3))
    part = settled(3)
    pleft[:HALF] = part[:HALF].astype(BF)
    arrived(qa.at[second], c_recv.at[1])
    pleft[HALF:] = (part[HALF:] + qa[HALF:].astype(F32)).astype(BF)
    send(pleft, qr, c_send.at[3], c_recv.at[3], near(0, 3))
    part = settled(1)
    pr[HALF:] = part[HALF:].astype(BF)
    arrived(qa.at[first], c_recv.at[0])
    pr[:HALF] = (part[:HALF] + qa[:HALF].astype(F32)).astype(BF)
    send(pr, ql, c_send.at[2], c_recv.at[2], near(0, 1))
    part = settled(0)
    arrived(ql, c_recv.at[2])
    part += ql[...].astype(F32)
    arrived(qr, c_recv.at[3])
    part += qr[...].astype(F32)
    rowsf[...] = part
    tz[...] = part.astype(BF)
    for k in range(1, NZ):
        to_rows = pl.ds(pl.multiple_of(((z + k) % NZ) * R, R), R)
        send(tz.at[to_rows], rz.at[k - 1], zz_send.at[k - 1], zz_recv.at[k - 1], place((z + k) % NZ, core, x, y))
    total = rowsf[z_rows, :]
    for k in range(1, NZ):
        arrived(rz.at[k - 1], zz_recv.at[k - 1])
        total += rz[k - 1].astype(F32)
    out_ref[...] = (values + total).astype(BF)
    for copy in started:
        copy.wait_send()


def feed_forward(stream, norm_gain, active, up_weight, down_weight):
    cols = stream.shape[1]
    width = 16 * cols
    vmem = pl.BlockSpec(memory_space=pltpu.VMEM)
    hbm = pl.BlockSpec(memory_space=pl.ANY)
    dma = pltpu.SemaphoreType.DMA
    full = pltpu.VMEM((ROWS, cols), BF)
    four = pltpu.VMEM((4, ROWS, cols), BF)
    return pl.pallas_call(
        ffn_kernel,
        out_shape=jax.ShapeDtypeStruct((R, cols), BF),
        in_specs=[vmem, vmem, vmem, hbm, hbm],
        out_specs=vmem,
        scratch_shapes=[
            pltpu.VMEM((4, 4, ROWS, cols), BF),
            pltpu.VMEM((2, width, 128), BF),
            pltpu.VMEM((256, width), BF),
            pltpu.VMEM((16, 2, 128), F32),
            pltpu.VMEM((ROWS, cols), F32),
            four, four, four, four, four, four,
            full, full, full, full, full, full, full,
            pltpu.VMEM((NZ - 1, R, cols), BF),
            dma((2,)), dma((2,)), dma((2,)),
            dma((15,)), dma((15,)),
            dma((NZ - 1,)), dma((NZ - 1,)),
            dma((4,)), dma((4,)),
            dma((4, 4)), dma((4, 4)),
            dma((2, 4)), dma((2, 4)), dma((2, 4)), dma((2, 4)),
            dma((4,)), dma((4,)),
            dma((NZ - 1,)), dma((NZ - 1,)),
        ],
        compiler_params=pltpu.CompilerParams(
            collective_id=0, has_side_effects=True, vmem_limit_bytes=56 * 1024 * 1024
        ),
        name="gather_ffn_scatter",
    )(stream, norm_gain.reshape(16, cols), active, up_weight, down_weight)


def shards(
    resid, query, key_new, value_new, key_cache, value_cache, lengths, norm_gain, active, up_weight, down_weight
):
    stream = attend(resid, query, key_new, value_new, key_cache, value_cache, lengths)
    return feed_forward(stream, norm_gain, active, up_weight, down_weight)


def solution(mesh):
    placed = (
        P("attn", ("ffn", "grp")),
        P("attn", ("ffn", "grp")),
        P("attn", ("ffn", "grp")),
        P("attn", ("ffn", "grp")),
        P("attn", None, ("ffn", "grp")),
        P("attn", None, ("ffn", "grp")),
        P("attn"),
        P(),
        P(),
        P(None, ("attn", "ffn", "grp")),
        P(("attn", "ffn", "grp"), None),
    )
    return jax.shard_map(
        shards, mesh=mesh, in_specs=placed, out_specs=P("attn", ("ffn", "grp")), check_vma=False
    )
```

```python
import jax
import jax.numpy as jnp
from jax import lax
from jax.experimental import pallas as pl
from jax.experimental.pallas import tpu as pltpu
from jax.sharding import PartitionSpec as P

MESH = pl.DeviceIdType.MESH
HD = 128
BF = jnp.bfloat16
F32 = jnp.float32
NT = (((1,), (1,)), ((), ()))
R = 16
NZ = 8
ROWS = R * NZ
HALF = ROWS // 2
QUART = HALF // 2
DIST = (0, 1, 7, 2, 6, 3, 5, 4)
STEP = 4


def layer_kernel(
    resid_ref, q_ref, kn_ref, vn_ref, k_ref, v_ref, len_ref, gain_ref, active_ref, up_ref, down_ref, out_ref,
    resid_s, q_s, kn_s, vn_s, k_s, v_s, len_s, gain_s, active_s, qf, knf, vnf, att,
    xbuf, wu, wd, stats,
    ya, yr, yl, ra, rl, rr, pa, pr, pleft, qa, ql, qr, tz, rz,
    in_sem, k_sem, v_sem, w_loc, w_send, w_recv, st_send, st_recv, z_send, z_recv, p1_send, p1_recv, p2_send, p2_recv,
    a_send, a_recv, b_send, b_recv, c_send, c_recv, zz_send, zz_recv,
):
    attn, ffn, grp = lax.axis_index("attn"), lax.axis_index("ffn"), lax.axis_index("grp")
    z, core = attn // 2, attn % 2
    x, y = ffn // 2, (ffn % 2) * 2 + grp
    other = 1 - core
    p1 = x * other + y * core
    p2 = y * other + x * core
    cols = resid_ref.shape[1]
    width = 16 * cols

    def place(z_at, core_at, x_at, y_at):
        return (z_at * 2 + core_at, x_at * 2 + y_at // 2, y_at % 2)

    def near(i, j):
        q2, q1 = (p2 + i) % 4, (p1 + j) % 4
        return place(z, core, q1 * other + q2 * core, q2 * other + q1 * core)

    def along_z(k):
        return place((z + k) % NZ, core, x, y)

    def group(i, j):
        q2, q1 = (p2 + i) % 4, (p1 + j) % 4
        return (q1 * other + q2 * core) * 4 + q2 * other + q1 * core

    def slot(i, j):
        return xbuf.at[(p2 + i) % 4, (p1 + j) % 4]

    started = []

    def send(src, dst, s_sem, r_sem, device):
        copy = pltpu.make_async_remote_copy(
            src_ref=src, dst_ref=dst, send_sem=s_sem, recv_sem=r_sem, device_id=device, device_id_type=MESH
        )
        copy.start()
        started.append(copy)

    def arrived(dst, r_sem):
        pltpu.make_async_remote_copy(
            src_ref=dst, dst_ref=dst, send_sem=r_sem, recv_sem=r_sem, device_id=near(0, 1), device_id_type=MESH
        ).wait_recv()

    def fetch(src, dst, sem):
        copy = pltpu.make_async_copy(src, dst, sem)
        copy.start()
        return copy

    small = [
        fetch(src, dst, in_sem.at[n])
        for n, (src, dst) in enumerate(
            [(q_ref, q_s), (kn_ref, kn_s), (len_ref, len_s), (vn_ref, vn_s), (resid_ref, resid_s),
             (gain_ref, gain_s), (active_ref, active_s)]
        )
    ]
    steps = [pl.ds(n * STEP, STEP) for n in range(R // STEP)]
    keys_in = [fetch(k_ref.at[rows], k_s.at[rows], k_sem.at[n]) for n, rows in enumerate(steps)]
    values_in = [fetch(v_ref.at[rows], v_s.at[rows], v_sem.at[n]) for n, rows in enumerate(steps)]

    plane = [(i, j) for i in range(4) for j in range(4) if (i, j) != (0, 0)]
    barrier = pltpu.get_barrier_semaphore()
    partner = place(z, other, x, y)
    for i, j in plane:
        pl.semaphore_signal(barrier, inc=1, device_id=near(i, j), device_id_type=MESH)
    for k in range(1, NZ):
        pl.semaphore_signal(barrier, inc=1, device_id=along_z(k), device_id_type=MESH)
    pl.semaphore_signal(barrier, inc=1, device_id=partner, device_id_type=MESH)

    scale = HD ** (-0.5)
    head_of = lax.broadcasted_iota(jnp.int32, (8, cols), 1) // HD
    mine_head = head_of == lax.broadcasted_iota(jnp.int32, (8, cols), 0)
    position = lax.broadcasted_iota(jnp.int32, (8, HD), 1)
    for copy in small[:3]:
        copy.wait()
    qf[...] = q_s[...].astype(F32)
    knf[...] = kn_s[...].astype(F32)
    weights, own_weights = [], []
    for n in range(R // STEP):
        requests = range(n * STEP, (n + 1) * STEP)
        heads = [jnp.where(mine_head, qf[r : r + 1, :], 0.0) for r in requests]
        own = [
            jnp.exp(jnp.sum(head * knf[r : r + 1, :], axis=1, keepdims=True) * scale)
            for r, head in zip(requests, heads)
        ]
        keys_in[n].wait()
        scores = [
            lax.dot_general(head.astype(BF), k_s[r], NT, preferred_element_type=F32) * scale
            for r, head in zip(requests, heads)
        ]
        expo = [jnp.where(position < len_s[r], jnp.exp(score), 0.0) for r, score in zip(requests, scores)]
        denom = [jnp.sum(e, axis=1, keepdims=True) + o for e, o in zip(expo, own)]
        weights += [(e / d).astype(BF) for e, d in zip(expo, denom)]
        own_weights += [(o / d).astype(BF).astype(F32) for o, d in zip(own, denom)]
    pl.semaphore_wait(barrier, len(plane) + NZ)
    up_here = fetch(up_ref, wu.at[core], w_loc.at[0])
    down_rows = pl.ds(pl.multiple_of(core * 128, 128), 128)
    down_other = pl.ds(pl.multiple_of(other * 128, 128), 128)
    send(up_ref, wu.at[core], w_send.at[0], w_recv.at[0], partner)
    for copy in small[3:]:
        copy.wait()
    vnf[...] = vn_s[...].astype(F32)
    for n in range(R // STEP):
        requests = range(n * STEP, (n + 1) * STEP)
        values_in[n].wait()
        mixed = [
            jnp.dot(weights[r], v_s[r], preferred_element_type=F32) + own_weights[r] * vnf[r : r + 1, :]
            for r in requests
        ]
        for r, part in zip(requests, mixed):
            att[r : r + 1, :] = jnp.sum(jnp.where(mine_head, part, 0.0), axis=0, keepdims=True)
    values = (resid_s[...].astype(F32) + att[...]).astype(BF).astype(F32)

    eye = (
        lax.broadcasted_iota(jnp.int32, (R, 128), 0) == lax.broadcasted_iota(jnp.int32, (R, 128), 1)
    ).astype(F32)
    own_mean = jnp.mean(values, axis=1, keepdims=True)
    off = values - own_mean
    own_sq = jnp.sum(off * off, axis=1, keepdims=True)
    here = stats.at[group(0, 0)]
    here[0:1, :] = jnp.sum(own_mean * eye, axis=0, keepdims=True)
    here[1:2, :] = jnp.sum(own_sq * eye, axis=0, keepdims=True)
    for n, (i, j) in enumerate(plane):
        send(here, here, st_send.at[n], st_recv.at[n], near(i, j))
    down_here = fetch(down_ref, wd.at[down_rows], w_loc.at[1])
    send(down_ref, wd.at[down_rows], w_send.at[1], w_recv.at[1], partner)

    block0 = z * 32 + group(0, 0)
    hit0 = jnp.max((active_s[...] == block0).astype(F32), axis=1, keepdims=True)
    hit1 = jnp.max((active_s[...] == block0 + 16).astype(F32), axis=1, keepdims=True)
    spans = active_s.shape[0]
    hits = jnp.concatenate([jnp.broadcast_to(hit0, (spans, 128)), jnp.broadcast_to(hit1, (spans, 128))], axis=1)
    row_at = lax.broadcasted_iota(jnp.int32, (ROWS, spans), 0)
    span_at = lax.broadcasted_iota(jnp.int32, (ROWS, spans), 1)
    lie = row_at // R
    away = jnp.where(lie % 2 == 1, (lie + 1) // 2, (NZ - lie // 2) % NZ)
    span_of = (((z + away) % NZ) * 2 + core) * 4 + (row_at % R) // 4
    row_mask = jnp.dot((span_of == span_at).astype(BF), hits.astype(BF), preferred_element_type=F32)
    gain = jnp.concatenate([gain_s[pl.ds(group(0, 0) * 6 + n, 1), :] for n in range(cols // 128)], axis=1)

    for n, (i, j) in enumerate(plane):
        arrived(stats.at[group(4 - i, 4 - j)], st_recv.at[n])
    means, squares = stats[:, 0, :], stats[:, 1, :]
    mean_all = jnp.sum(means, axis=0, keepdims=True) * (1.0 / 16)
    gap = means - mean_all
    var_all = (jnp.sum(squares, axis=0, keepdims=True) + cols * jnp.sum(gap * gap, axis=0, keepdims=True)) * (
        1.0 / width
    )
    mean_row = jnp.sum(mean_all * eye, axis=1, keepdims=True)
    rstd_row = jnp.sum(lax.rsqrt(var_all + 1e-05) * eye, axis=1, keepdims=True)
    mine = slot(0, 0)
    mine[0:R, :] = ((values - mean_row) * rstd_row * gain).astype(BF)

    def lies(k):
        return pl.ds(DIST.index(k) * R, R)

    for k in (1, 7, 6, 2, 5, 3, 4):
        send(mine.at[0:R], mine.at[lies(NZ - k)], z_send.at[k - 1], z_recv.at[k - 1], along_z(k))

    part_rows = [pl.ds(h * HALF, HALF) for h in range(2)]
    first = [pl.ds(h * HALF, QUART) for h in range(2)]
    second = [pl.ds(h * HALF + QUART, QUART) for h in range(2)]

    def copy1(j, rows, n, h, to):
        send(slot(0, j).at[rows], slot(0, j).at[rows], p1_send.at[n, h], p1_recv.at[n, h], near(0, to))

    def copy2(i, j, rows, n, h, to):
        send(slot(i, j).at[rows], slot(i, j).at[rows], p2_send.at[n, h, j], p2_recv.at[n, h, j], near(to, 0))

    def spread(j, h):
        copy2(0, j, part_rows[h], 0, h, 1)
        copy2(0, j, part_rows[h], 1, h, 3)

    def relay1(h):
        arrived(slot(0, 3).at[part_rows[h]], p1_recv.at[0, h])
        copy1(3, first[h], 2, h, 1)
        spread(3, h)
        arrived(slot(0, 1).at[part_rows[h]], p1_recv.at[1, h])
        copy1(1, second[h], 3, h, 3)
        spread(1, h)

    def opposite1(h):
        arrived(slot(0, 2).at[first[h]], p1_recv.at[2, h])
        arrived(slot(0, 2).at[second[h]], p1_recv.at[3, h])
        spread(2, h)

    def relay2(j, h):
        arrived(slot(3, j).at[part_rows[h]], p2_recv.at[0, h, j])
        copy2(3, j, first[h], 2, h, 1)
        arrived(slot(1, j).at[part_rows[h]], p2_recv.at[1, h, j])
        copy2(1, j, second[h], 3, h, 3)

    def opposite2(j, h):
        arrived(slot(2, j).at[first[h]], p2_recv.at[2, h, j])
        arrived(slot(2, j).at[second[h]], p2_recv.at[3, h, j])

    def up(i, j):
        rows = pl.ds(pl.multiple_of(group(i, j) * cols, 128), cols)
        both = jnp.concatenate([wu[0, rows, :], wu[1, rows, :]], axis=1)
        return jnp.dot(slot(i, j)[...], both, preferred_element_type=F32)

    for h, distances in enumerate(((1, 7, 2), (6, 3, 5, 4))):
        for k in distances:
            arrived(mine.at[lies(k)], z_recv.at[NZ - k - 1])
        copy1(0, part_rows[h], 0, h, 1)
        copy1(0, part_rows[h], 1, h, 3)
        spread(0, h)
    relay1(0)
    relay2(0, 0)
    relay1(1)
    opposite1(0)
    relay2(0, 1)
    opposite1(1)
    relay2(3, 0)
    relay2(1, 0)
    up_here.wait()
    arrived(wu.at[other], w_recv.at[0])
    before = up(0, 0) + up(0, 3) + up(0, 1) + up(0, 2)
    relay2(3, 1)
    before += up(3, 0) + up(1, 0)
    relay2(1, 1)
    before += up(3, 3) + up(1, 3)
    relay2(2, 0)
    before += up(3, 1) + up(1, 1)
    relay2(2, 1)
    before += up(3, 2) + up(1, 2)
    for j in (0, 3, 1, 2):
        opposite2(j, 0)
        opposite2(j, 1)
        before += up(2, j)
    hidden = (jnp.maximum(before, 0.0) * row_mask).astype(BF)

    down_here.wait()
    arrived(wd.at[down_other], w_recv.at[1])
    back = (2, 3, 1, 0)

    def down(i, j, h):
        columns = pl.ds(pl.multiple_of(group(i, j) * cols, 128), cols)
        return jnp.dot(hidden[h * HALF : (h + 1) * HALF], wd[:, columns], preferred_element_type=F32)

    for h in (1, 0):
        for j in back:
            ya[j, part_rows[h], :] = down(2, j, h).astype(BF)
            send(ya.at[j, first[h]], ra.at[j, first[h]], a_send.at[0, h, j], a_recv.at[0, h, j], near(1, 0))
            send(ya.at[j, second[h]], ra.at[j, second[h]], a_send.at[1, h, j], a_recv.at[1, h, j], near(3, 0))
    for h in (1, 0):
        for j in back:
            part = down(1, j, h)
            arrived(ra.at[j, first[h]], a_recv.at[0, h, j])
            yr[j, first[h], :] = (part[:QUART] + ra[j, first[h], :].astype(F32)).astype(BF)
            yr[j, second[h], :] = part[QUART:].astype(BF)
            send(yr.at[j, part_rows[h]], rl.at[j, part_rows[h]], b_send.at[0, h, j], b_recv.at[0, h, j], near(1, 0))
            part = down(3, j, h)
            arrived(ra.at[j, second[h]], a_recv.at[1, h, j])
            yl[j, first[h], :] = part[:QUART].astype(BF)
            yl[j, second[h], :] = (part[QUART:] + ra[j, second[h], :].astype(F32)).astype(BF)
            send(yl.at[j, part_rows[h]], rr.at[j, part_rows[h]], b_send.at[1, h, j], b_recv.at[1, h, j], near(3, 0))

    def settled(j, h):
        part = down(0, j, h)
        arrived(rl.at[j, part_rows[h]], b_recv.at[0, h, j])
        part += rl[j, part_rows[h], :].astype(F32)
        arrived(rr.at[j, part_rows[h]], b_recv.at[1, h, j])
        return part + rr[j, part_rows[h], :].astype(F32)

    def settle_opposite(h):
        pa[part_rows[h], :] = settled(2, h).astype(BF)
        send(pa.at[first[h]], qa.at[first[h]], c_send.at[0, h], c_recv.at[0, h], near(0, 1))
        send(pa.at[second[h]], qa.at[second[h]], c_send.at[1, h], c_recv.at[1, h], near(0, 3))

    def settle_beside(h):
        part = settled(3, h)
        arrived(qa.at[second[h]], c_recv.at[1, h])
        pleft[first[h], :] = part[:QUART].astype(BF)
        pleft[second[h], :] = (part[QUART:] + qa[second[h], :].astype(F32)).astype(BF)
        send(pleft.at[part_rows[h]], qr.at[part_rows[h]], c_send.at[3, h], c_recv.at[3, h], near(0, 3))
        part = settled(1, h)
        arrived(qa.at[first[h]], c_recv.at[0, h])
        pr[first[h], :] = (part[:QUART] + qa[first[h], :].astype(F32)).astype(BF)
        pr[second[h], :] = part[QUART:].astype(BF)
        send(pr.at[part_rows[h]], ql.at[part_rows[h]], c_send.at[2, h], c_recv.at[2, h], near(0, 1))

    def settle_own(h, distances):
        part = settled(0, h)
        arrived(ql.at[part_rows[h]], c_recv.at[2, h])
        part += ql[part_rows[h], :].astype(F32)
        arrived(qr.at[part_rows[h]], c_recv.at[3, h])
        part += qr[part_rows[h], :].astype(F32)
        tz[part_rows[h], :] = part.astype(BF)
        for k in distances:
            send(tz.at[lies(k)], rz.at[k - 1], zz_send.at[k - 1], zz_recv.at[k - 1], along_z(k))
        return part

    settle_opposite(1)
    settle_beside(1)
    settle_opposite(0)
    settle_own(1, (4, 3, 5, 6))
    settle_beside(0)
    total = settle_own(0, (2, 1, 7))[:R] + values
    for k in (4, 3, 5, 6, 2, 1, 7):
        arrived(rz.at[k - 1], zz_recv.at[k - 1])
        total += rz[k - 1].astype(F32)
    out_ref[...] = total.astype(BF)
    for copy in started:
        copy.wait_send()


def layer(resid, query, key_new, value_new, key_cache, value_cache, lengths, norm_gain, active, up, down):
    cols = resid.shape[1]
    width = 16 * cols
    hbm = pl.BlockSpec(memory_space=pl.ANY)
    dma = pltpu.SemaphoreType.DMA
    row = pltpu.VMEM((R, cols), BF)
    row32 = pltpu.VMEM((R, cols), F32)
    cache = pltpu.VMEM((R, 128, cols), BF)
    full = pltpu.VMEM((ROWS, cols), BF)
    four = pltpu.VMEM((4, ROWS, cols), BF)
    return pl.pallas_call(
        layer_kernel,
        out_shape=jax.ShapeDtypeStruct((R, cols), BF),
        in_specs=[hbm] * 11,
        out_specs=pl.BlockSpec(memory_space=pltpu.VMEM),
        scratch_shapes=[
            row, row, row, row, cache, cache,
            pltpu.SMEM((R,), jnp.int32),
            pltpu.VMEM((norm_gain.shape[0] // 128, 128), F32),
            pltpu.VMEM(active.shape, jnp.int32),
            row32, row32, row32, row32,
            pltpu.VMEM((4, 4, ROWS, cols), BF),
            pltpu.VMEM((2, width, 128), BF),
            pltpu.VMEM((256, width), BF),
            pltpu.VMEM((16, 2, 128), F32),
            four, four, four, four, four, four,
            full, full, full, full, full, full, full,
            pltpu.VMEM((NZ - 1, R, cols), BF),
            dma((7,)), dma((R // STEP,)), dma((R // STEP,)),
            dma((2,)), dma((2,)), dma((2,)),
            dma((15,)), dma((15,)),
            dma((NZ - 1,)), dma((NZ - 1,)),
            dma((4, 2)), dma((4, 2)),
            dma((4, 2, 4)), dma((4, 2, 4)),
            dma((2, 2, 4)), dma((2, 2, 4)), dma((2, 2, 4)), dma((2, 2, 4)),
            dma((4, 2)), dma((4, 2)),
            dma((NZ - 1,)), dma((NZ - 1,)),
        ],
        compiler_params=pltpu.CompilerParams(
            collective_id=0, has_side_effects=True, vmem_limit_bytes=60 * 1024 * 1024
        ),
        name="layer",
    )(resid, query, key_new, value_new, key_cache, value_cache, lengths, norm_gain.reshape(-1, 128), active, up, down)


def shards(
    resid, query, key_new, value_new, key_cache, value_cache, lengths, norm_gain, active, up_weight, down_weight
):
    return layer(
        resid, query, key_new, value_new, key_cache, value_cache, lengths, norm_gain, active, up_weight, down_weight
    )


def solution(mesh):
    placed = (
        P("attn", ("ffn", "grp")),
        P("attn", ("ffn", "grp")),
        P("attn", ("ffn", "grp")),
        P("attn", ("ffn", "grp")),
        P("attn", None, ("ffn", "grp")),
        P("attn", None, ("ffn", "grp")),
        P("attn"),
        P(),
        P(),
        P(None, ("attn", "ffn", "grp")),
        P(("attn", "ffn", "grp"), None),
    )
    return jax.shard_map(
        shards, mesh=mesh, in_specs=placed, out_specs=P("attn", ("ffn", "grp")), check_vma=False
    )
```

```python
import jax
import jax.numpy as jnp
from jax import lax
from jax.experimental import pallas as pl
from jax.experimental.pallas import tpu as pltpu
from jax.sharding import PartitionSpec as P

MESH = pl.DeviceIdType.MESH
HD = 128
BF = jnp.bfloat16
F32 = jnp.float32
NT = (((1,), (1,)), ((), ()))
R = 16
NZ = 8
ROWS = R * NZ
DIST = (0, 1, 7, 2, 6, 3, 5, 4)
STEP = 4
CB = 128
CHUNKS = (slice(0, 16), slice(16, 64), slice(64, 128))


def layer_kernel(
    resid_ref, q_ref, kn_ref, vn_ref, k_ref, v_ref, len_ref, gain_ref, active_ref, up_ref, down_ref, out_ref,
    resid_s, q_s, kn_s, vn_s, k_s, v_s, len_s, gain_s, active_s, qf, knf, vnf, att,
    xbuf, wu, wd, stats,
    gb, us, zst, yf, ya, yr, yl, ra, rlr, ps, qs, tz, rz, xb, pb, zs, zr, tb, rxy,
    in_sem, k_sem, v_sem, w_loc, w_send, w_recv, st_send, st_recv, sz_send, sz_recv, z_send, z_recv, p1_send, p1_recv, p2_send, p2_recv, p2o_recv,
    a_send, a_recv, b_send, b_recv, c_send, c_recv, zz_send, zz_recv,
    xy_send, xy_recv, ring_send, ring_recv, back_send, back_recv, xyb_send, xyb_recv,
):
    attn, ffn, grp = lax.axis_index("attn"), lax.axis_index("ffn"), lax.axis_index("grp")
    z, core = attn // 2, attn % 2
    x, y = ffn // 2, (ffn % 2) * 2 + grp
    other = 1 - core
    p1 = x * other + y * core
    p2 = y * other + x * core
    cols = resid_ref.shape[1]
    ca = cols - CB
    width = 16 * cols

    def place(z_at, core_at, x_at, y_at):
        return (z_at * 2 + core_at, x_at * 2 + y_at // 2, y_at % 2)

    def near(i, j):
        q2, q1 = (p2 + i) % 4, (p1 + j) % 4
        return place(z, core, q1 * other + q2 * core, q2 * other + q1 * core)

    def along_z(k):
        return place((z + k) % NZ, core, x, y)

    def group(i, j):
        q2, q1 = (p2 + i) % 4, (p1 + j) % 4
        return (q1 * other + q2 * core) * 4 + q2 * other + q1 * core

    def slot(i, j):
        return xbuf.at[(p2 + i) % 4, (p1 + j) % 4]

    def send(src, dst, s_sem, r_sem, device):
        copy = pltpu.make_async_remote_copy(
            src_ref=src, dst_ref=dst, send_sem=s_sem, recv_sem=r_sem, device_id=device, device_id_type=MESH
        )
        copy.start()

    def sent(src, s_sem):
        pltpu.make_async_remote_copy(
            src_ref=src, dst_ref=src, send_sem=s_sem, recv_sem=s_sem, device_id=near(0, 1), device_id_type=MESH
        ).wait_send()

    def arrived(dst, r_sem):
        pltpu.make_async_remote_copy(
            src_ref=dst, dst_ref=dst, send_sem=r_sem, recv_sem=r_sem, device_id=near(0, 1), device_id_type=MESH
        ).wait_recv()

    def fetch(src, dst, sem):
        copy = pltpu.make_async_copy(src, dst, sem)
        copy.start()
        return copy

    small = [
        fetch(src, dst, in_sem.at[n])
        for n, (src, dst) in enumerate(
            [(q_ref, q_s), (kn_ref, kn_s), (len_ref, len_s), (vn_ref, vn_s), (resid_ref, resid_s),
             (gain_ref, gain_s), (active_ref, active_s)]
        )
    ]
    steps = [pl.ds(n * STEP, STEP) for n in range(R // STEP)]
    keys_in = [fetch(k_ref.at[rows], k_s.at[rows], k_sem.at[n]) for n, rows in enumerate(steps)]
    values_in = [fetch(v_ref.at[rows], v_s.at[rows], v_sem.at[n]) for n, rows in enumerate(steps)]

    plane = [(i, j) for i in range(4) for j in range(4) if (i, j) != (0, 0)]
    barrier = pltpu.get_barrier_semaphore()
    partner = place(z, other, x, y)
    for i, j in plane:
        pl.semaphore_signal(barrier, inc=1, device_id=near(i, j), device_id_type=MESH)
    for k in range(1, NZ):
        pl.semaphore_signal(barrier, inc=1, device_id=along_z(k), device_id_type=MESH)
    pl.semaphore_signal(barrier, inc=1, device_id=partner, device_id_type=MESH)

    scale = HD ** (-0.5)
    head_of = lax.broadcasted_iota(jnp.int32, (8, cols), 1) // HD
    mine_head = head_of == lax.broadcasted_iota(jnp.int32, (8, cols), 0)
    position = lax.broadcasted_iota(jnp.int32, (8, HD), 1)
    for copy in small[:3]:
        copy.wait()
    qf[...] = q_s[...].astype(F32)
    knf[...] = kn_s[...].astype(F32)
    weights, own_weights = [], []
    for n in range(R // STEP):
        requests = range(n * STEP, (n + 1) * STEP)
        heads = [jnp.where(mine_head, qf[r : r + 1, :], 0.0) for r in requests]
        own = [
            jnp.exp(jnp.sum(head * knf[r : r + 1, :], axis=1, keepdims=True) * scale)
            for r, head in zip(requests, heads)
        ]
        keys_in[n].wait()
        scores = [
            lax.dot_general(head.astype(BF), k_s[r], NT, preferred_element_type=F32) * scale
            for r, head in zip(requests, heads)
        ]
        expo = [jnp.where(position < len_s[r], jnp.exp(score), 0.0) for r, score in zip(requests, scores)]
        denom = [jnp.sum(e, axis=1, keepdims=True) + o for e, o in zip(expo, own)]
        weights += [(e / d).astype(BF) for e, d in zip(expo, denom)]
        own_weights += [(o / d).astype(BF).astype(F32) for o, d in zip(own, denom)]
    pl.semaphore_wait(barrier, len(plane) + NZ)
    up_here = fetch(up_ref, wu.at[core], w_loc.at[0])
    down_rows = pl.ds(pl.multiple_of(core * 128, 128), 128)
    down_other = pl.ds(pl.multiple_of(other * 128, 128), 128)
    send(up_ref, wu.at[core], w_send.at[0], w_recv.at[0], partner)
    for copy in small[3:]:
        copy.wait()
    vnf[...] = vn_s[...].astype(F32)
    for n in range(R // STEP):
        requests = range(n * STEP, (n + 1) * STEP)
        values_in[n].wait()
        mixed = [
            jnp.dot(weights[r], v_s[r], preferred_element_type=F32) + own_weights[r] * vnf[r : r + 1, :]
            for r in requests
        ]
        for r, part in zip(requests, mixed):
            att[r : r + 1, :] = jnp.sum(jnp.where(mine_head, part, 0.0), axis=0, keepdims=True)
    values = (resid_s[...].astype(F32) + att[...]).astype(BF).astype(F32)

    def lies(k):
        return pl.ds(DIST.index(k) * R, R)

    gain = jnp.concatenate([gain_s[pl.ds(group(0, 0) * 6 + n, 1), :] for n in range(cols // 128)], axis=1)
    own_mean = jnp.mean(values, axis=1, keepdims=True)
    off = values - own_mean
    scaled = (off * gain).astype(BF)
    mine = slot(0, 0)
    mine[0:R, :] = scaled[:, :ca]
    mine_b = xb.at[0, p2 * 4 + p1]
    mine_b[...] = scaled[:, ca:]

    def copy1(t, c):
        rows = CHUNKS[c]
        send(slot(0, 0).at[rows], slot(0, 0).at[rows], p1_send, p1_recv.at[t - 1, c], near(0, t))

    def copy2(i, j, rows, n, c, to):
        if rows.start < rows.stop:
            sem = p2_recv.at[n, c, j] if n < 2 else p2o_recv.at[j]
            send(slot(i, j).at[rows], slot(i, j).at[rows], p2_send, sem, near(to, 0))

    def spread(j, c):
        copy2(0, j, CHUNKS[c], 0, c, 1)
        copy2(0, j, CHUNKS[c], 1, c, 3)

    def own_part(c):
        for t in (1, 3, 2):
            copy1(t, c)
        spread(0, c)

    def to_z(distances):
        for k in distances:
            send(mine.at[0:R], mine.at[lies(NZ - k)], z_send, z_recv.at[0 if k in (1, 7, 6) else 1], along_z(k))

    to_z((1, 7, 6))
    own_part(0)
    to_z((2, 5, 3, 4))
    for i, j in plane:
        send(mine_b, mine_b, xy_send, xy_recv, near(i, j))

    lane = lax.broadcasted_iota(jnp.int32, (R, 128), 1)
    line = lax.broadcasted_iota(jnp.int32, (R, 128), 0)
    g_here = group(0, 0)
    eye = (lane == (g_here % 8) * 16 + line).astype(F32)
    own_sq = jnp.sum(off * off, axis=1, keepdims=True)
    here = stats.at[g_here]
    here[0:1, :] = jnp.sum(own_mean * eye, axis=0, keepdims=True)
    here[1:2, :] = jnp.sum(own_sq * eye, axis=0, keepdims=True)
    for i, j in plane:
        send(here, here, st_send, st_recv, near(i, j))
    down_here = fetch(down_ref, wd.at[down_rows], w_loc.at[1])
    send(down_ref, wd.at[down_rows], w_send.at[1], w_recv.at[1], partner)

    for g in range(16):
        row = jnp.concatenate([gain_s[g * 6 + n : g * 6 + n + 1, :] for n in range(cols // 128)], axis=1)
        high = row.astype(BF).astype(F32)
        upper = lax.broadcasted_iota(jnp.int32, (16, cols), 0) < 8
        gb[g] = jnp.where(upper, high, row - high).astype(BF)

    block0 = z * 32 + group(0, 0)
    hit0 = jnp.max((active_s[...] == block0).astype(F32), axis=1, keepdims=True)
    hit1 = jnp.max((active_s[...] == block0 + 16).astype(F32), axis=1, keepdims=True)
    spans = active_s.shape[0]
    hits = jnp.concatenate([jnp.broadcast_to(hit0, (spans, 128)), jnp.broadcast_to(hit1, (spans, 128))], axis=1)
    row_at = lax.broadcasted_iota(jnp.int32, (ROWS, spans), 0)
    span_at = lax.broadcasted_iota(jnp.int32, (ROWS, spans), 1)
    lie = row_at // R
    away = jnp.where(lie % 2 == 1, (lie + 1) // 2, (NZ - lie // 2) % NZ)
    span_of = (((z + away) % NZ) * 2 + core) * 4 + (row_at % R) // 4
    row_mask = jnp.dot((span_of == span_at).astype(BF), hits.astype(BF), preferred_element_type=F32)
    def by_right(j, c):
        return (slice(0, 16 - 16 * (j % 2)), slice(16, 32 + 16 * (j % 2)), slice(64, 96))[c]

    def by_left(j, c):
        return (slice(16 - 16 * (j % 2), 16), slice(32 + 16 * (j % 2), 64), slice(96, 128))[c]

    def relay1(c):
        for j in (3, 1, 2):
            arrived(slot(0, j).at[CHUNKS[c]], p1_recv.at[3 - j, c])
            spread(j, c)

    def relay2(j, c):
        arrived(slot(3, j).at[CHUNKS[c]], p2_recv.at[0, c, j])
        copy2(3, j, by_right(j, c), 2, c, 1)
        arrived(slot(1, j).at[CHUNKS[c]], p2_recv.at[1, c, j])
        copy2(1, j, by_left(j, c), 3, c, 3)

    def opposite2(j):
        arrived(slot(2, j), p2o_recv.at[j])

    def up(i, j):
        g = group(i, j)
        rows = pl.ds(pl.multiple_of(g * cols, 128), ca)
        both = jnp.concatenate([wu[0, rows, :], wu[1, rows, :]], axis=1)
        lines = jnp.concatenate([slot(i, j)[...], gb[g, :, :ca]], axis=0)
        part = jnp.dot(lines, both, preferred_element_type=F32)
        us[g] = part[ROWS:]
        return part[:ROWS]

    pieces = [slice(0, 8), slice(8, 16)]

    def ring_on(way, step, piece):
        at, to = ((NZ - step) % NZ, NZ - step - 1) if way == 0 else (step, step + 1)
        send(
            xb.at[at, pieces[piece]], xb.at[to, pieces[piece]],
            ring_send, ring_recv.at[way, step, piece], along_z(1 if way == 0 else NZ - 1),
        )

    def ring_in(way, step, piece):
        at = NZ - step if way == 0 else step
        arrived(xb.at[at, pieces[piece]], ring_recv.at[way, step - 1, piece])

    def ring_start():
        arrived(xb.at[0, 0:15], xy_recv)
        for piece in range(2):
            for way in range(2):
                ring_on(way, 0, piece)

    def ring_relay(step, piece):
        for way in range(2):
            ring_in(way, step, piece)
            if step < 3 or piece == way:
                ring_on(way, step, piece)

    def ring_end():
        ring_in(0, 4, 0)
        ring_in(1, 4, 1)

    def up_b(q2, q1):
        g = (q1 * other + q2 * core) * 4 + q2 * other + q1 * core
        rows = pl.ds(pl.multiple_of(g * cols + ca, 128), CB)
        both = jnp.concatenate([wu[0, rows, :], wu[1, rows, :]], axis=1)
        lines = jnp.concatenate([xb[k, q2 * 4 + q1] for k in DIST] + [gb[g, :, ca:]], axis=0)
        part = jnp.dot(lines, both, preferred_element_type=F32)
        us[g] = us[g] + part[ROWS:]
        return part[:ROWS]

    relay1(0)
    arrived(mine.at[CHUNKS[1]], z_recv.at[0])
    own_part(1)
    ring_start()
    arrived(mine.at[CHUNKS[2]], z_recv.at[1])
    own_part(2)
    relay2(0, 0)
    relay1(1)
    ring_relay(1, 0)
    arrived(stats.at[0:15], st_recv)
    for half in range(2):
        zst[0, 2 * half : 2 * half + 2, :] = jnp.sum(stats[8 * half : 8 * half + 8], axis=0)
    for k in range(1, NZ):
        send(zst.at[0], zst.at[NZ - k], sz_send, sz_recv, along_z(k))
    ring_relay(1, 1)
    relay2(3, 0)
    relay2(1, 0)
    relay2(2, 0)
    relay1(2)
    relay2(0, 1)
    ring_relay(2, 0)
    relay2(3, 1)
    relay2(1, 1)
    ring_relay(2, 1)
    relay2(2, 1)
    relay2(0, 2)
    up_here.wait()
    arrived(wu.at[other], w_recv.at[0])
    before = up(0, 0) + up(0, 3)
    ring_relay(3, 0)
    relay2(3, 2)
    before += up(0, 1) + up(0, 2)
    ring_relay(3, 1)
    relay2(1, 2)
    before += up(3, 0) + up(1, 0)
    relay2(2, 2)
    before += up(3, 3) + up(1, 3)
    before += up(3, 1) + up(1, 1)
    before += up(3, 2) + up(1, 2)

    arrived(zst.at[1:NZ], sz_recv)
    own_lane = lane % 16 == line
    mean_at, square_at = [
        [jnp.concatenate([jnp.where(own_lane, zst[k, 2 * half + n : 2 * half + n + 1, :], 0.0) for k in DIST], axis=0) for half in range(2)]
        for n in range(2)
    ]
    mean_row = jnp.sum(mean_at[0] + mean_at[1], axis=1, keepdims=True) * (1.0 / 16)
    lanes = lax.broadcasted_iota(jnp.int32, (ROWS, 128), 1) % 16 == lax.broadcasted_iota(jnp.int32, (ROWS, 128), 0) % 16
    gaps = [jnp.where(lanes, part - mean_row, 0.0) for part in mean_at]
    var_row = jnp.sum(
        square_at[0] + square_at[1] + cols * (gaps[0] * gaps[0] + gaps[1] * gaps[1]), axis=1, keepdims=True
    ) * (1.0 / width)
    rstd_row = lax.rsqrt(var_row + 1e-05)

    for j in (0, 3, 1, 2):
        opposite2(j)
        before += up(2, j)
    ring_end()
    for q2 in range(4):
        for q1 in range(4):
            before += up_b(q2, q1)
    for half in range(2):
        gains = []
        for g in range(8 * half, 8 * half + 8):
            both = us[g, :8, :] + us[g, 8:, :]
            gains += [both, both]
        before += jnp.dot(
            gaps[half], jnp.concatenate(gains, axis=0), preferred_element_type=F32, precision=lax.Precision.HIGHEST
        )
    hidden = (jnp.maximum(before * rstd_row, 0.0) * row_mask).astype(BF)

    down_here.wait()
    arrived(wd.at[down_other], w_recv.at[1])
    back = (2, 3, 1, 0)

    def down(i, j):
        columns = pl.ds(pl.multiple_of(group(i, j) * cols, 128), ca)
        return jnp.dot(hidden, wd[:, columns], preferred_element_type=F32)

    def pass_on(src, dst, j, rows, c, to, s_sem, r_sem):
        if rows.start < rows.stop:
            send(src.at[j, rows], dst.at[j, rows], s_sem, r_sem.at[c, j], near(to, 0))

    def with_arrived(base, j, rows, out):
        if rows.start < rows.stop:
            out[j, rows, :] = (yf[base, j, rows, :] + ra[j, rows, :].astype(F32)).astype(BF)

    def alone(base, j, rows, out):
        if rows.start < rows.stop:
            out[j, rows, :] = yf[base, j, rows, :].astype(BF)

    def start_back(c):
        for j in back:
            pass_on(ya, ra, j, by_right(j, c), c, 1, a_send, a_recv)
            pass_on(ya, ra, j, by_left(j, c), c, 3, a_send, a_recv)

    def beside_back(j, c):
        alone(0, j, by_left(j, c), yr)
        alone(1, j, by_right(j, c), yl)
        arrived(ra.at[j, CHUNKS[c]], a_recv.at[c, j])
        with_arrived(0, j, by_right(j, c), yr)
        pass_on(yr, rlr.at[0], j, CHUNKS[c], c, 1, b_send.at[0], b_recv)
        with_arrived(1, j, by_left(j, c), yl)
        pass_on(yl, rlr.at[1], j, CHUNKS[c], c, 3, b_send.at[1], b_recv)

    def ring_back(way, k, piece):
        away = k if way == 0 else NZ - k
        part = pb[away, pieces[piece]]
        if k < 3 or (k == 3 and piece == way):
            arrived(zr.at[way, k, pieces[piece]], back_recv.at[way, k, piece])
            part += zr[way, k, pieces[piece]].astype(F32)
        zs[way, k - 1, pieces[piece]] = part.astype(BF)
        send(
            zs.at[way, k - 1, pieces[piece]], zr.at[way, k - 1, pieces[piece]],
            back_send, back_recv.at[way, k - 1, piece], along_z(1 if way == 0 else NZ - 1),
        )

    for j in back:
        ya[j] = down(2, j).astype(BF)
    start_back(2)
    for q2 in range(4):
        for q1 in range(4):
            g = (q1 * other + q2 * core) * 4 + q2 * other + q1 * core
            columns = pl.ds(pl.multiple_of(g * cols + ca, 128), CB)
            part = jnp.dot(hidden, wd[:, columns], preferred_element_type=F32)
            for n, k in enumerate(DIST):
                pb[k, q2 * 4 + q1] = part[n * R : (n + 1) * R]
    ring_back(0, 4, 0)
    ring_back(1, 4, 1)
    ring_back(0, 3, 1)
    ring_back(1, 3, 0)
    start_back(1)
    start_back(0)
    for j in back:
        yf[0, j] = down(1, j)
        yf[1, j] = down(3, j)
        beside_back(j, 2)
    ring_back(0, 3, 0)
    ring_back(1, 3, 1)
    for j in back:
        beside_back(j, 1)
    ring_back(0, 2, 1)
    ring_back(1, 2, 0)
    for j in back:
        beside_back(j, 0)
    ring_back(0, 2, 0)
    ring_back(1, 2, 1)
    for j in back:
        yf[2, j] = down(0, j)

    def settled(j, c):
        rows = CHUNKS[c]
        arrived(rlr.at[:, j, rows], b_recv.at[c, j])
        return yf[2, j, rows, :] + rlr[0, j, rows, :].astype(F32) + rlr[1, j, rows, :].astype(F32)

    def settle(c):
        rows = CHUNKS[c]
        for j in (2, 3, 1):
            ps[j - 1, rows, :] = settled(j, c).astype(BF)
            send(ps.at[j - 1, rows], qs.at[j - 1, rows], c_send, c_recv.at[c], near(0, j))

    def settle_own(c):
        rows = CHUNKS[c]
        part = settled(0, c)
        arrived(qs.at[:, rows], c_recv.at[c])
        for j in (3, 1, 2):
            part += qs[j - 1, rows, :].astype(F32)
        return part

    def to_owners(c, distances):
        rows = CHUNKS[c]
        tz[rows, :] = settle_own(c).astype(BF)
        for k in distances:
            send(tz.at[lies(k)], rz.at[k - 1], zz_send, zz_recv, along_z(k))

    settle(2)
    ring_back(0, 1, 1)
    ring_back(1, 1, 0)
    settle(1)
    to_owners(2, (4, 3, 5, 6))
    ring_back(0, 1, 0)
    ring_back(1, 1, 1)
    settle(0)
    to_owners(1, (2, 1, 7))
    for piece in range(2):
        for way in range(2):
            arrived(zr.at[way, 0, pieces[piece]], back_recv.at[way, 0, piece])
    whole = pb[0] + zr[0, 0].astype(F32) + zr[1, 0].astype(F32)
    pb[0] = whole
    tb[...] = whole.astype(BF)
    for n, (i, j) in enumerate(plane):
        send(tb.at[(p2 + i) % 4 * 4 + (p1 + j) % 4], rxy.at[n], xyb_send, xyb_recv, near(i, j))
    total = settle_own(0) + values[:, :ca]
    total_b = pb[0, p2 * 4 + p1] + values[:, ca:]
    arrived(rz, zz_recv)
    for k in range(1, NZ):
        total += rz[k - 1].astype(F32)
    out_ref[:, :ca] = total.astype(BF)
    arrived(rxy, xyb_recv)
    for n in range(len(plane)):
        total_b += rxy[n].astype(F32)
    out_ref[:, ca:] = total_b.astype(BF)
    for src, sem in (
        (up_ref, w_send.at[0]), (down_ref, w_send.at[1]), (stats.at[0:15], st_send), (zst.at[1:NZ], sz_send),
        (mine.at[0 : ROWS - R], z_send), (xbuf.at[0, 0:3], p1_send), (xbuf.at[0:3], p2_send), (xb.at[0, 0:15], xy_send),
        (xb.at[0:7], ring_send), (xb.at[0:7], back_send), (ya, a_send), (yr, b_send.at[0]), (yl, b_send.at[1]),
        (ps, c_send), (rz, zz_send), (rxy, xyb_send),
    ):
        sent(src, sem)


def layer(resid, query, key_new, value_new, key_cache, value_cache, lengths, norm_gain, active, up, down):
    cols = resid.shape[1]
    width = 16 * cols
    hbm = pl.BlockSpec(memory_space=pl.ANY)
    dma = pltpu.SemaphoreType.DMA
    row = pltpu.VMEM((R, cols), BF)
    row32 = pltpu.VMEM((R, cols), F32)
    cache = pltpu.VMEM((R, 128, cols), BF)
    ca = cols - CB
    full = pltpu.VMEM((ROWS, ca), BF)
    four = pltpu.VMEM((4, ROWS, ca), BF)
    ring = (16, R, CB)
    one = dma(())
    return pl.pallas_call(
        layer_kernel,
        out_shape=jax.ShapeDtypeStruct((R, cols), BF),
        in_specs=[hbm] * 11,
        out_specs=pl.BlockSpec(memory_space=pltpu.VMEM),
        scratch_shapes=[
            row, row, row, row, cache, cache,
            pltpu.SMEM((R,), jnp.int32),
            pltpu.VMEM((norm_gain.shape[0] // 128, 128), F32),
            pltpu.VMEM(active.shape, jnp.int32),
            row32, row32, row32, row32,
            pltpu.VMEM((4, 4, ROWS, ca), BF),
            pltpu.VMEM((2, width, 128), BF),
            pltpu.VMEM((256, width), BF),
            pltpu.VMEM((16, 2, 128), F32),
            pltpu.VMEM((16, 16, cols), BF),
            pltpu.VMEM((16, 16, 256), F32),
            pltpu.VMEM((NZ, 4, 128), F32),
            pltpu.VMEM((3, 4, ROWS, ca), F32),
            four, four, four, four,
            pltpu.VMEM((2, 4, ROWS, ca), BF),
            pltpu.VMEM((3, ROWS, ca), BF),
            pltpu.VMEM((3, ROWS, ca), BF),
            full,
            pltpu.VMEM((NZ - 1, R, ca), BF),
            pltpu.VMEM((NZ,) + ring, BF),
            pltpu.VMEM((NZ,) + ring, F32),
            pltpu.VMEM((2, 4) + ring, BF),
            pltpu.VMEM((2, 4) + ring, BF),
            pltpu.VMEM(ring, BF),
            pltpu.VMEM((15, R, CB), BF),
            dma((7,)), dma((R // STEP,)), dma((R // STEP,)), dma((2,)), dma((2,)), dma((2,)),
            one, one, one, one, one, dma((2,)),
            one, dma((3, 3)), one, dma((2, 3, 4)), dma((4,)),
            one, dma((3, 4)), dma((2,)), dma((3, 4)), one, dma((3,)), one, one,
            one, one, one, dma((2, 4, 2)), one, dma((2, 4, 2)), one, one,
        ],
        compiler_params=pltpu.CompilerParams(
            collective_id=0, has_side_effects=True, vmem_limit_bytes=60 * 1024 * 1024
        ),
        name="layer",
    )(resid, query, key_new, value_new, key_cache, value_cache, lengths, norm_gain.reshape(-1, 128), active, up, down)


def shards(
    resid, query, key_new, value_new, key_cache, value_cache, lengths, norm_gain, active, up_weight, down_weight
):
    return layer(
        resid, query, key_new, value_new, key_cache, value_cache, lengths, norm_gain, active, up_weight, down_weight
    )


def solution(mesh):
    placed = (
        P("attn", ("ffn", "grp")),
        P("attn", ("ffn", "grp")),
        P("attn", ("ffn", "grp")),
        P("attn", ("ffn", "grp")),
        P("attn", None, ("ffn", "grp")),
        P("attn", None, ("ffn", "grp")),
        P("attn"),
        P(),
        P(),
        P(None, ("attn", "ffn", "grp")),
        P(("attn", "ffn", "grp"), None),
    )
    return jax.shard_map(
        shards, mesh=mesh, in_specs=placed, out_specs=P("attn", ("ffn", "grp")), check_vma=False
    )
```

```python
import functools

import jax
import jax.numpy as jnp
from jax import lax
from jax.experimental import pallas as pl
from jax.experimental.pallas import tpu as pltpu
from jax.sharding import PartitionSpec as P

MESH = pl.DeviceIdType.MESH
HD = 128
BF = jnp.bfloat16
F32 = jnp.float32
NT = (((1,), (1,)), ((), ()))
R = 16
NZ = 8
ROWS = R * NZ
DIST = (0, 1, 7, 2, 6, 3, 5, 4)
STEP = 4
CBS = ((0, 0), (256, 384))
CB = max(CBS[0] + CBS[1])
CHUNKS = (slice(0, 16), slice(16, 80), slice(80, 128))


def layer_kernel(
    resid_ref, q_ref, kn_ref, vn_ref, k_ref, v_ref, len_ref, gain_ref, active_ref, up_ref, down_ref, out_ref,
    resid_s, q_s, kn_s, vn_s, k_s, v_s, len_s, gain_s, active_s, qf, knf, vnf, att,
    xbuf, wu, wd, stats,
    gb, us, zst, yf_s, ya_s, yr_s, yl_s, ra_s, rlr_s, ps_s, qs_s, tz_s, rz_s, xb_s, pb_s, zs_s, zr_s, tb_s, rxy_s,
    in_sem, k_sem, v_sem, w_loc, w_send, w_recv, st_send, st_recv, sz_send, sz_recv, z_send, z_recv, p1_send, p1_recv, p2_send, p2_recv, p2o_recv,
    a_send, a_recv, b_send, b_recv, c_send, c_recv, zz_send, zz_recv,
    xy_send, xy_recv, ring_send, ring_recv, back_send, back_recv, xyb_send, xyb_recv,
):
    attn, ffn, grp = lax.axis_index("attn"), lax.axis_index("ffn"), lax.axis_index("grp")
    z, core = attn // 2, attn % 2
    x, y = ffn // 2, (ffn % 2) * 2 + grp
    other = 1 - core
    p1 = x * other + y * core
    p2 = y * other + x * core
    cols = resid_ref.shape[1]
    width = 16 * cols

    def place(z_at, core_at, x_at, y_at):
        return (z_at * 2 + core_at, x_at * 2 + y_at // 2, y_at % 2)

    def near(i, j):
        q2, q1 = (p2 + i) % 4, (p1 + j) % 4
        return place(z, core, q1 * other + q2 * core, q2 * other + q1 * core)

    def along_z(k):
        return place((z + k) % NZ, core, x, y)

    def group(i, j):
        q2, q1 = (p2 + i) % 4, (p1 + j) % 4
        return (q1 * other + q2 * core) * 4 + q2 * other + q1 * core

    def send(src, dst, s_sem, r_sem, device):
        copy = pltpu.make_async_remote_copy(
            src_ref=src, dst_ref=dst, send_sem=s_sem, recv_sem=r_sem, device_id=device, device_id_type=MESH
        )
        copy.start()

    def sent(src, s_sem):
        pltpu.make_async_remote_copy(
            src_ref=src, dst_ref=src, send_sem=s_sem, recv_sem=s_sem, device_id=near(0, 1), device_id_type=MESH
        ).wait_send()

    def arrived(dst, r_sem):
        pltpu.make_async_remote_copy(
            src_ref=dst, dst_ref=dst, send_sem=r_sem, recv_sem=r_sem, device_id=near(0, 1), device_id_type=MESH
        ).wait_recv()

    def fetch(src, dst, sem):
        copy = pltpu.make_async_copy(src, dst, sem)
        copy.start()
        return copy

    small = [
        fetch(src, dst, in_sem.at[n])
        for n, (src, dst) in enumerate(
            [(q_ref, q_s), (kn_ref, kn_s), (len_ref, len_s), (vn_ref, vn_s), (resid_ref, resid_s),
             (gain_ref, gain_s), (active_ref, active_s)]
        )
    ]
    steps = [pl.ds(n * STEP, STEP) for n in range(R // STEP)]
    keys_in = [fetch(k_ref.at[rows], k_s.at[rows], k_sem.at[n]) for n, rows in enumerate(steps)]
    values_in = [fetch(v_ref.at[rows], v_s.at[rows], v_sem.at[n]) for n, rows in enumerate(steps)]

    plane = [(i, j) for i in range(4) for j in range(4) if (i, j) != (0, 0)]
    barrier = pltpu.get_barrier_semaphore()
    partner = place(z, other, x, y)
    for i, j in plane:
        pl.semaphore_signal(barrier, inc=1, device_id=near(i, j), device_id_type=MESH)
    for k in range(1, NZ):
        pl.semaphore_signal(barrier, inc=1, device_id=along_z(k), device_id_type=MESH)
    pl.semaphore_signal(barrier, inc=1, device_id=partner, device_id_type=MESH)

    scale = HD ** (-0.5)
    head_of = lax.broadcasted_iota(jnp.int32, (8, cols), 1) // HD
    mine_head = head_of == lax.broadcasted_iota(jnp.int32, (8, cols), 0)
    position = lax.broadcasted_iota(jnp.int32, (8, HD), 1)
    for copy in small[:3]:
        copy.wait()
    qf[...] = q_s[...].astype(F32)
    knf[...] = kn_s[...].astype(F32)
    weights, own_weights = [], []
    for n in range(R // STEP):
        requests = range(n * STEP, (n + 1) * STEP)
        heads = [jnp.where(mine_head, qf[r : r + 1, :], 0.0) for r in requests]
        own = [
            jnp.exp(jnp.sum(head * knf[r : r + 1, :], axis=1, keepdims=True) * scale)
            for r, head in zip(requests, heads)
        ]
        keys_in[n].wait()
        scores = [
            lax.dot_general(head.astype(BF), k_s[r], NT, preferred_element_type=F32) * scale
            for r, head in zip(requests, heads)
        ]
        expo = [jnp.where(position < len_s[r], jnp.exp(score), 0.0) for r, score in zip(requests, scores)]
        denom = [jnp.sum(e, axis=1, keepdims=True) + o for e, o in zip(expo, own)]
        weights += [(e / d).astype(BF) for e, d in zip(expo, denom)]
        own_weights += [(o / d).astype(BF).astype(F32) for o, d in zip(own, denom)]
    pl.semaphore_wait(barrier, len(plane) + NZ)
    up_here = fetch(up_ref, wu.at[core], w_loc.at[0])
    down_rows = pl.ds(pl.multiple_of(core * 128, 128), 128)
    down_other = pl.ds(pl.multiple_of(other * 128, 128), 128)
    send(up_ref, wu.at[core], w_send.at[0], w_recv.at[0], partner)
    for copy in small[3:]:
        copy.wait()
    vnf[...] = vn_s[...].astype(F32)
    for n in range(R // STEP):
        requests = range(n * STEP, (n + 1) * STEP)
        values_in[n].wait()
        mixed = [
            jnp.dot(weights[r], v_s[r], preferred_element_type=F32) + own_weights[r] * vnf[r : r + 1, :]
            for r in requests
        ]
        for r, part in zip(requests, mixed):
            att[r : r + 1, :] = jnp.sum(jnp.where(mine_head, part, 0.0), axis=0, keepdims=True)
    values = (resid_s[...].astype(F32) + att[...]).astype(BF).astype(F32)

    def exchange(cb, kb):
        ca, ka = cols - cb, cols - kb
        xa = xbuf.at[:, :, :, 0:ca]
        ya, yr, yl, ra = [ref.at[:, :, 0:ka] for ref in (ya_s, yr_s, yl_s, ra_s)]
        yf, rlr = [ref.at[:, :, :, 0:ka] for ref in (yf_s, rlr_s)]
        ps, qs, rz = [ref.at[:, :, 0:ka] for ref in (ps_s, qs_s, rz_s)]
        tz = tz_s.at[:, 0:ka]
        if cb:
            xb = xb_s.at[:, :, :, 0:cb]
        if kb:
            pb, zs, tb, rxy = pb_s.at[:, :, :, 0:kb], zs_s.at[:, :, :, 0:kb], tb_s.at[:, :, 0:kb], rxy_s.at[:, :, 0:kb]
            zr = zr_s.at[:, :, :, :, 0:kb]

        def slot(i, j):
            return xa.at[(p2 + i) % 4, (p1 + j) % 4]

        def lies(k):
            return pl.ds(DIST.index(k) * R, R)

        gain = jnp.concatenate([gain_s[pl.ds(group(0, 0) * 6 + n, 1), :] for n in range(cols // 128)], axis=1)
        own_mean = jnp.mean(values, axis=1, keepdims=True)
        off = values - own_mean
        scaled = (off * gain).astype(BF)
        mine = slot(0, 0)
        mine[0:R, :] = scaled[:, :ca]
        if cb:
            mine_b = xb.at[0, p2 * 4 + p1]
            mine_b[...] = scaled[:, ca:]

        def copy1(t, c):
            rows = CHUNKS[c]
            send(slot(0, 0).at[rows], slot(0, 0).at[rows], p1_send, p1_recv.at[t - 1, c], near(0, t))

        def copy2(i, j, rows, n, c, to):
            if rows.start < rows.stop:
                sem = p2_recv.at[n, c, j] if n < 2 else p2o_recv.at[j]
                send(slot(i, j).at[rows], slot(i, j).at[rows], p2_send, sem, near(to, 0))

        def spread(j, c):
            copy2(0, j, CHUNKS[c], 0, c, 1)
            copy2(0, j, CHUNKS[c], 1, c, 3)

        def own_part(c):
            for t in (1, 3, 2):
                copy1(t, c)
            spread(0, c)

        def to_z(distances):
            for k in distances:
                send(mine.at[0:R], mine.at[lies(NZ - k)], z_send, z_recv.at[0 if k in (1, 7, 6, 2) else 1], along_z(k))

        to_z((6, 2, 1, 7))
        own_part(0)
        to_z((4, 5, 3))
        for i, j in plane if cb else []:
            send(mine_b, mine_b, xy_send, xy_recv, near(i, j))

        lane = lax.broadcasted_iota(jnp.int32, (R, 128), 1)
        line = lax.broadcasted_iota(jnp.int32, (R, 128), 0)
        g_here = group(0, 0)
        eye = (lane == (g_here % 8) * 16 + line).astype(F32)
        own_sq = jnp.sum(off * off, axis=1, keepdims=True)
        here = stats.at[g_here]
        here[0:1, :] = jnp.sum(own_mean * eye, axis=0, keepdims=True)
        here[1:2, :] = jnp.sum(own_sq * eye, axis=0, keepdims=True)
        for i, j in plane:
            send(here, here, st_send, st_recv, near(i, j))
        down_here = fetch(down_ref, wd.at[down_rows], w_loc.at[1])
        send(down_ref, wd.at[down_rows], w_send.at[1], w_recv.at[1], partner)

        for g in range(16):
            row = jnp.concatenate([gain_s[g * 6 + n : g * 6 + n + 1, :] for n in range(cols // 128)], axis=1)
            high = row.astype(BF).astype(F32)
            upper = lax.broadcasted_iota(jnp.int32, (16, cols), 0) < 8
            gb[g] = jnp.where(upper, high, row - high).astype(BF)

        block0 = z * 32 + group(0, 0)
        hit0 = jnp.max((active_s[...] == block0).astype(F32), axis=1, keepdims=True)
        hit1 = jnp.max((active_s[...] == block0 + 16).astype(F32), axis=1, keepdims=True)
        spans = active_s.shape[0]
        hits = jnp.concatenate([jnp.broadcast_to(hit0, (spans, 128)), jnp.broadcast_to(hit1, (spans, 128))], axis=1)
        row_at = lax.broadcasted_iota(jnp.int32, (ROWS, spans), 0)
        span_at = lax.broadcasted_iota(jnp.int32, (ROWS, spans), 1)
        lie = row_at // R
        away = jnp.where(lie % 2 == 1, (lie + 1) // 2, (NZ - lie // 2) % NZ)
        span_of = (((z + away) % NZ) * 2 + core) * 4 + (row_at % R) // 4
        row_mask = jnp.dot((span_of == span_at).astype(BF), hits.astype(BF), preferred_element_type=F32)
        def by_right(j, c):
            return (slice(0, 16 - 16 * (j % 2)), slice(16, 48), slice(80, 96 + 16 * (j % 2)))[c]

        def by_left(j, c):
            return (slice(16 - 16 * (j % 2), 16), slice(48, 80), slice(96 + 16 * (j % 2), 128))[c]

        def relay1(c):
            for j in (3, 1, 2):
                arrived(slot(0, j).at[CHUNKS[c]], p1_recv.at[3 - j, c])
                spread(j, c)

        def relay2(j, c):
            arrived(slot(3, j).at[CHUNKS[c]], p2_recv.at[0, c, j])
            copy2(3, j, by_right(j, c), 2, c, 1)
            arrived(slot(1, j).at[CHUNKS[c]], p2_recv.at[1, c, j])
            copy2(1, j, by_left(j, c), 3, c, 3)

        def opposite2(j):
            arrived(slot(2, j), p2o_recv.at[j])

        def up(i, j):
            g = group(i, j)
            rows = pl.ds(pl.multiple_of(g * cols, 128), ca)
            both = jnp.concatenate([wu[0, rows, :], wu[1, rows, :]], axis=1)
            if i == 2:
                return jnp.dot(slot(i, j)[...], both, preferred_element_type=F32)
            lines = jnp.concatenate([slot(i, j)[...], gb[g, :, :ca]], axis=0)
            part = jnp.dot(lines, both, preferred_element_type=F32)
            us[g] = part[ROWS:]
            return part[:ROWS]

        def gain_part(i, j):
            g = group(i, j)
            rows = pl.ds(pl.multiple_of(g * cols, 128), ca)
            both = jnp.concatenate([wu[0, rows, :], wu[1, rows, :]], axis=1)
            us[g] = jnp.dot(gb[g, :, :ca], both, preferred_element_type=F32)

        pieces = [slice(0, 8), slice(8, 16)]

        def ring_on(way, step, piece):
            at, to = ((NZ - step) % NZ, NZ - step - 1) if way == 0 else (step, step + 1)
            send(
                xb.at[at, pieces[piece]], xb.at[to, pieces[piece]],
                ring_send, ring_recv.at[way, step, piece], along_z(1 if way == 0 else NZ - 1),
            )

        def ring_in(way, step, piece):
            at = NZ - step if way == 0 else step
            arrived(xb.at[at, pieces[piece]], ring_recv.at[way, step - 1, piece])

        def ring_start():
            if not cb:
                return
            arrived(xb.at[0, 0:15], xy_recv)
            for piece in range(2):
                for way in range(2):
                    ring_on(way, 0, piece)

        def ring_relay(step, piece):
            if not cb:
                return
            for way in range(2):
                ring_in(way, step, piece)
                if step < 3 or piece == way:
                    ring_on(way, step, piece)

        def ring_end():
            ring_in(0, 4, 0)
            ring_in(1, 4, 1)

        def up_b(q2, q1):
            g = (q1 * other + q2 * core) * 4 + q2 * other + q1 * core
            rows = pl.ds(pl.multiple_of(g * cols + ca, 128), cb)
            both = jnp.concatenate([wu[0, rows, :], wu[1, rows, :]], axis=1)
            lines = jnp.concatenate([xb[k, q2 * 4 + q1] for k in DIST] + [gb[g, :, ca:]], axis=0)
            part = jnp.dot(lines, both, preferred_element_type=F32)
            us[g] = us[g] + part[ROWS:]
            return part[:ROWS]

        relay1(0)
        arrived(mine.at[CHUNKS[1]], z_recv.at[0])
        own_part(1)
        ring_start()
        arrived(mine.at[CHUNKS[2]], z_recv.at[1])
        own_part(2)
        relay2(0, 0)
        relay1(1)
        ring_relay(1, 0)
        arrived(stats.at[0:15], st_recv)
        for half in range(2):
            zst[0, 2 * half : 2 * half + 2, :] = jnp.sum(stats[8 * half : 8 * half + 8], axis=0)
        for k in range(1, NZ):
            send(zst.at[0], zst.at[NZ - k], sz_send, sz_recv, along_z(k))
        ring_relay(1, 1)
        relay2(3, 0)
        relay2(1, 0)
        relay2(2, 0)
        relay1(2)
        relay2(0, 1)
        ring_relay(2, 0)
        relay2(3, 1)
        relay2(1, 1)
        ring_relay(2, 1)
        relay2(2, 1)
        relay2(0, 2)
        ring_relay(3, 0)
        relay2(3, 2)
        ring_relay(3, 1)
        relay2(1, 2)
        relay2(2, 2)
        up_here.wait()
        arrived(wu.at[other], w_recv.at[0])
        before = up(0, 0) + up(0, 3)
        before += up(0, 1) + up(0, 2)
        before += up(3, 0) + up(1, 0)
        before += up(3, 3) + up(1, 3)
        before += up(3, 1) + up(1, 1)
        before += up(3, 2) + up(1, 2)

        arrived(zst.at[1:NZ], sz_recv)
        own_lane = lane % 16 == line
        mean_at, square_at = [
            [jnp.concatenate([jnp.where(own_lane, zst[k, 2 * half + n : 2 * half + n + 1, :], 0.0) for k in DIST], axis=0) for half in range(2)]
            for n in range(2)
        ]
        mean_row = jnp.sum(mean_at[0] + mean_at[1], axis=1, keepdims=True) * (1.0 / 16)
        lanes = lax.broadcasted_iota(jnp.int32, (ROWS, 128), 1) % 16 == lax.broadcasted_iota(jnp.int32, (ROWS, 128), 0) % 16
        gaps = [jnp.where(lanes, part - mean_row, 0.0) for part in mean_at]
        var_row = jnp.sum(
            square_at[0] + square_at[1] + cols * (gaps[0] * gaps[0] + gaps[1] * gaps[1]), axis=1, keepdims=True
        ) * (1.0 / width)
        rstd_row = lax.rsqrt(var_row + 1e-05)

        for j in range(4):
            gain_part(2, j)
        if cb:
            ring_end()
        for q in range(16) if cb else []:
            before += up_b(q // 4, q % 4)
        for half in range(2):
            gains = []
            for g in range(8 * half, 8 * half + 8):
                both = us[g, :8, :] + us[g, 8:, :]
                gains += [both, both]
            before += jnp.dot(
                gaps[half], jnp.concatenate(gains, axis=0), preferred_element_type=F32, precision=lax.Precision.HIGHEST
            )
        for j in (0, 3, 1, 2):
            opposite2(j)
            before += up(2, j)
        hidden = (jnp.maximum(before * rstd_row, 0.0) * row_mask).astype(BF)

        down_here.wait()
        arrived(wd.at[down_other], w_recv.at[1])
        back = (2, 3, 1, 0)

        def down(i, j):
            columns = pl.ds(pl.multiple_of(group(i, j) * cols, 128), ka)
            return jnp.dot(hidden, wd[:, columns], preferred_element_type=F32)

        def pass_on(src, dst, j, rows, c, to, s_sem, r_sem):
            if rows.start < rows.stop:
                send(src.at[j, rows], dst.at[j, rows], s_sem, r_sem.at[c, j], near(to, 0))

        def with_arrived(base, j, rows, out):
            if rows.start < rows.stop:
                out[j, rows, :] = (yf[base, j, rows, :] + ra[j, rows, :].astype(F32)).astype(BF)

        def alone(base, j, rows, out):
            if rows.start < rows.stop:
                out[j, rows, :] = yf[base, j, rows, :].astype(BF)

        def start_back(c, slots):
            for j in slots:
                pass_on(ya, ra, j, by_right(j, c), c, 1, a_send, a_recv)
                pass_on(ya, ra, j, by_left(j, c), c, 3, a_send, a_recv)

        def beside_back(j, c):
            alone(0, j, by_left(j, c), yr)
            alone(1, j, by_right(j, c), yl)
            arrived(ra.at[j, CHUNKS[c]], a_recv.at[c, j])
            with_arrived(0, j, by_right(j, c), yr)
            pass_on(yr, rlr.at[0], j, CHUNKS[c], c, 1, b_send.at[0], b_recv)
            with_arrived(1, j, by_left(j, c), yl)
            pass_on(yl, rlr.at[1], j, CHUNKS[c], c, 3, b_send.at[1], b_recv)

        def ring_back(way, k, piece):
            if not kb:
                return
            away = k if way == 0 else NZ - k
            part = pb[away, pieces[piece]]
            if k < 3 or (k == 3 and piece == way):
                arrived(zr.at[way, k, pieces[piece]], back_recv.at[way, k, piece])
                part += zr[way, k, pieces[piece]].astype(F32)
            zs[way * 4 + k - 1, pieces[piece]] = part.astype(BF)
            send(
                zs.at[way * 4 + k - 1, pieces[piece]], zr.at[way, k - 1, pieces[piece]],
                back_send, back_recv.at[way, k - 1, piece], along_z(1 if way == 0 else NZ - 1),
            )

        for j in back:
            ya[j] = down(2, j).astype(BF)
            start_back(2, (j,))
        start_back(0, back)
        start_back(1, back)
        for q2, q1 in [(q // 4, q % 4) for q in range(16)] if kb else []:
            g = (q1 * other + q2 * core) * 4 + q2 * other + q1 * core
            columns = pl.ds(pl.multiple_of(g * cols + ka, 128), kb)
            part = jnp.dot(hidden, wd[:, columns], preferred_element_type=F32)
            for n, k in enumerate(DIST):
                pb[k, q2 * 4 + q1] = part[n * R : (n + 1) * R]
        ring_back(0, 4, 0)
        ring_back(1, 4, 1)
        ring_back(0, 3, 1)
        ring_back(1, 3, 0)
        for j in back:
            yf[0, j] = down(1, j)
            yf[1, j] = down(3, j)
            beside_back(j, 2)
        ring_back(0, 3, 0)
        ring_back(1, 3, 1)
        for j in back:
            beside_back(j, 1)
        ring_back(0, 2, 1)
        ring_back(1, 2, 0)
        for j in back:
            beside_back(j, 0)
        ring_back(0, 2, 0)
        ring_back(1, 2, 1)
        for j in back:
            yf[2, j] = down(0, j)

        def settled(j, c):
            rows = CHUNKS[c]
            arrived(rlr.at[:, j, rows], b_recv.at[c, j])
            return yf[2, j, rows, :] + rlr[0, j, rows, :].astype(F32) + rlr[1, j, rows, :].astype(F32)

        def settle(c):
            rows = CHUNKS[c]
            for j in (2, 3, 1):
                ps[j - 1, rows, :] = settled(j, c).astype(BF)
                send(ps.at[j - 1, rows], qs.at[j - 1, rows], c_send, c_recv.at[c], near(0, j))

        def settle_own(c):
            rows = CHUNKS[c]
            part = settled(0, c)
            arrived(qs.at[:, rows], c_recv.at[c])
            for j in (3, 1, 2):
                part += qs[j - 1, rows, :].astype(F32)
            return part

        def to_owners(c, distances):
            rows = CHUNKS[c]
            tz[rows, :] = settle_own(c).astype(BF)
            for k in distances:
                send(tz.at[lies(k)], rz.at[k - 1], zz_send, zz_recv, along_z(k))

        settle(2)
        ring_back(0, 1, 1)
        ring_back(1, 1, 0)
        settle(1)
        to_owners(2, (4, 3, 5))
        ring_back(0, 1, 0)
        ring_back(1, 1, 1)
        settle(0)
        to_owners(1, (2, 6, 1, 7))
        if kb:
            for piece in range(2):
                for way in range(2):
                    arrived(zr.at[way, 0, pieces[piece]], back_recv.at[way, 0, piece])
            whole = pb[0] + zr[0, 0].astype(F32) + zr[1, 0].astype(F32)
            pb[0] = whole
            tb[...] = whole.astype(BF)
            for n, (i, j) in enumerate(plane):
                send(tb.at[(p2 + i) % 4 * 4 + (p1 + j) % 4], rxy.at[n], xyb_send, xyb_recv, near(i, j))
        total = settle_own(0) + values[:, :ka]
        if kb:
            total_b = pb[0, p2 * 4 + p1] + values[:, ka:]
        arrived(rz, zz_recv)
        for k in range(1, NZ):
            total += rz[k - 1].astype(F32)
        out_ref[:, :ka] = total.astype(BF)
        if kb:
            arrived(rxy, xyb_recv)
            for n in range(len(plane)):
                total_b += rxy[n].astype(F32)
            out_ref[:, ka:] = total_b.astype(BF)
        for src, sem in (
            (up_ref, w_send.at[0]), (down_ref, w_send.at[1]), (stats.at[0:15], st_send), (zst.at[1:NZ], sz_send),
            (mine.at[0 : ROWS - R], z_send), (xa.at[0, 0:3], p1_send), (xa.at[0:3], p2_send), (ya, a_send), (yr, b_send.at[0]), (yl, b_send.at[1]),
            (ps, c_send), (rz, zz_send),
        ):
            sent(src, sem)
        for src, sem in ((xb.at[0, 0:15], xy_send), (xb.at[0:7], ring_send)) if cb else ():
            sent(src, sem)
        for src, sem in ((zs.at[0:7], back_send), (rxy, xyb_send)) if kb else ():
            sent(src, sem)

    for n in range(2):
        pl.when(core == n)(functools.partial(exchange, *CBS[n]))


def layer(resid, query, key_new, value_new, key_cache, value_cache, lengths, norm_gain, active, up, down):
    cols = resid.shape[1]
    width = 16 * cols
    hbm = pl.BlockSpec(memory_space=pl.ANY)
    dma = pltpu.SemaphoreType.DMA
    row = pltpu.VMEM((R, cols), BF)
    row32 = pltpu.VMEM((R, cols), F32)
    cache = pltpu.VMEM((R, 128, cols), BF)
    full = pltpu.VMEM((ROWS, cols), BF)
    four = pltpu.VMEM((4, ROWS, cols), BF)
    ring = (16, R, CB)
    one = dma(())
    return pl.pallas_call(
        layer_kernel,
        out_shape=jax.ShapeDtypeStruct((R, cols), BF),
        in_specs=[hbm] * 11,
        out_specs=pl.BlockSpec(memory_space=pltpu.VMEM),
        scratch_shapes=[
            row, row, row, row, cache, cache,
            pltpu.SMEM((R,), jnp.int32),
            pltpu.VMEM((norm_gain.shape[0] // 128, 128), F32),
            pltpu.VMEM(active.shape, jnp.int32),
            row32, row32, row32, row32,
            pltpu.VMEM((4, 4, ROWS, cols), BF),
            pltpu.VMEM((2, width, 128), BF),
            pltpu.VMEM((256, width), BF),
            pltpu.VMEM((16, 2, 128), F32),
            pltpu.VMEM((16, 16, cols), BF),
            pltpu.VMEM((16, 16, 256), F32),
            pltpu.VMEM((NZ, 4, 128), F32),
            pltpu.VMEM((3, 4, ROWS, cols), F32),
            four, four, four, four,
            pltpu.VMEM((2, 4, ROWS, cols), BF),
            pltpu.VMEM((3, ROWS, cols), BF),
            pltpu.VMEM((3, ROWS, cols), BF),
            full,
            pltpu.VMEM((NZ - 1, R, cols), BF),
            pltpu.VMEM((NZ,) + ring, BF),
            pltpu.VMEM((NZ,) + ring, F32),
            pltpu.VMEM((8,) + ring, BF),
            pltpu.VMEM((2, 4) + ring, BF),
            pltpu.VMEM(ring, BF),
            pltpu.VMEM((15, R, CB), BF),
            dma((7,)), dma((R // STEP,)), dma((R // STEP,)), dma((2,)), dma((2,)), dma((2,)),
            one, one, one, one, one, dma((2,)),
            one, dma((3, 3)), one, dma((2, 3, 4)), dma((4,)),
            one, dma((3, 4)), dma((2,)), dma((3, 4)), one, dma((3,)), one, one,
            one, one, one, dma((2, 4, 2)), one, dma((2, 4, 2)), one, one,
        ],
        compiler_params=pltpu.CompilerParams(
            collective_id=0, has_side_effects=True, vmem_limit_bytes=60 * 1024 * 1024
        ),
        name="layer",
    )(resid, query, key_new, value_new, key_cache, value_cache, lengths, norm_gain.reshape(-1, 128), active, up, down)


def shards(
    resid, query, key_new, value_new, key_cache, value_cache, lengths, norm_gain, active, up_weight, down_weight
):
    return layer(
        resid, query, key_new, value_new, key_cache, value_cache, lengths, norm_gain, active, up_weight, down_weight
    )


def solution(mesh):
    placed = (
        P("attn", ("ffn", "grp")),
        P("attn", ("ffn", "grp")),
        P("attn", ("ffn", "grp")),
        P("attn", ("ffn", "grp")),
        P("attn", None, ("ffn", "grp")),
        P("attn", None, ("ffn", "grp")),
        P("attn"),
        P(),
        P(),
        P(None, ("attn", "ffn", "grp")),
        P(("attn", "ffn", "grp"), None),
    )
    return jax.shard_map(
        shards, mesh=mesh, in_specs=placed, out_specs=P("attn", ("ffn", "grp")), check_vma=False
    )
```

```python
import functools

import jax
import jax.numpy as jnp
from jax import lax
from jax.experimental import pallas as pl
from jax.experimental.pallas import tpu as pltpu
from jax.sharding import PartitionSpec as P

MESH = pl.DeviceIdType.MESH
HD = 128
BF = jnp.bfloat16
F32 = jnp.float32
NT = (((1,), (1,)), ((), ()))
R = 16
NZ = 8
ROWS = R * NZ
DIST = (0, 1, 7, 2, 6, 3, 5, 4)
STEP = 4
CBS = ((0, 128), (256, 256))
CB = max(CBS[0] + CBS[1])
CHUNKS = (slice(0, 16), slice(16, 80), slice(80, 128))


def layer_kernel(
    resid_ref, q_ref, kn_ref, vn_ref, k_ref, v_ref, len_ref, gain_ref, active_ref, up_ref, down_ref, out_ref,
    resid_s, q_s, kn_s, vn_s, k_s, v_s, len_s, gain_s, active_s, qf, knf, vnf, att,
    xbuf, wu, wd, stats,
    gb, us, zst, yf_s, ya_s, yr_s, yl_s, ra_s, rlr_s, ps_s, qs_s, tz_s, rz_s, xb_s, pb_s, zs_s, zr_s, tb_s, rxy_s,
    in_sem, k_sem, v_sem, w_loc, w_send, w_recv, st_send, st_recv, sz_send, sz_recv, z_send, z_recv, p1_send, p1_recv, p2_send, p2_recv, p2o_recv,
    a_send, a_recv, b_send, b_recv, c_send, c_recv, zz_send, zz_recv,
    xy_send, xy_recv, ring_send, ring_recv, back_send, back_recv, xyb_send, xyb_recv,
):
    attn, ffn, grp = lax.axis_index("attn"), lax.axis_index("ffn"), lax.axis_index("grp")
    z, core = attn // 2, attn % 2
    x, y = ffn // 2, (ffn % 2) * 2 + grp
    other = 1 - core
    p1 = x * other + y * core
    p2 = y * other + x * core
    cols = resid_ref.shape[1]
    width = 16 * cols

    def place(z_at, core_at, x_at, y_at):
        return (z_at * 2 + core_at, x_at * 2 + y_at // 2, y_at % 2)

    def near(i, j):
        q2, q1 = (p2 + i) % 4, (p1 + j) % 4
        return place(z, core, q1 * other + q2 * core, q2 * other + q1 * core)

    def along_z(k):
        return place((z + k) % NZ, core, x, y)

    def group(i, j):
        q2, q1 = (p2 + i) % 4, (p1 + j) % 4
        return (q1 * other + q2 * core) * 4 + q2 * other + q1 * core

    def send(src, dst, s_sem, r_sem, device):
        copy = pltpu.make_async_remote_copy(
            src_ref=src, dst_ref=dst, send_sem=s_sem, recv_sem=r_sem, device_id=device, device_id_type=MESH
        )
        copy.start()

    def sent(src, s_sem):
        pltpu.make_async_remote_copy(
            src_ref=src, dst_ref=src, send_sem=s_sem, recv_sem=s_sem, device_id=near(0, 1), device_id_type=MESH
        ).wait_send()

    def arrived(dst, r_sem):
        pltpu.make_async_remote_copy(
            src_ref=dst, dst_ref=dst, send_sem=r_sem, recv_sem=r_sem, device_id=near(0, 1), device_id_type=MESH
        ).wait_recv()

    def fetch(src, dst, sem):
        copy = pltpu.make_async_copy(src, dst, sem)
        copy.start()
        return copy

    small = [
        fetch(src, dst, in_sem.at[n])
        for n, (src, dst) in enumerate(
            [(q_ref, q_s), (kn_ref, kn_s), (len_ref, len_s), (vn_ref, vn_s), (resid_ref, resid_s),
             (gain_ref, gain_s), (active_ref, active_s)]
        )
    ]
    steps = [pl.ds(n * STEP, STEP) for n in range(R // STEP)]
    keys_in = [fetch(k_ref.at[rows], k_s.at[rows], k_sem.at[n]) for n, rows in enumerate(steps)]
    values_in = [fetch(v_ref.at[rows], v_s.at[rows], v_sem.at[n]) for n, rows in enumerate(steps)]

    plane = [(i, j) for i in range(4) for j in range(4) if (i, j) != (0, 0)]
    barrier = pltpu.get_barrier_semaphore()
    partner = place(z, other, x, y)
    for i, j in plane:
        pl.semaphore_signal(barrier, inc=1, device_id=near(i, j), device_id_type=MESH)
    for k in range(1, NZ):
        pl.semaphore_signal(barrier, inc=1, device_id=along_z(k), device_id_type=MESH)
    pl.semaphore_signal(barrier, inc=1, device_id=partner, device_id_type=MESH)

    scale = HD ** (-0.5)
    head_of = lax.broadcasted_iota(jnp.int32, (8, cols), 1) // HD
    mine_head = head_of == lax.broadcasted_iota(jnp.int32, (8, cols), 0)
    position = lax.broadcasted_iota(jnp.int32, (8, HD), 1)
    for copy in small[:3]:
        copy.wait()
    qf[...] = q_s[...].astype(F32)
    knf[...] = kn_s[...].astype(F32)
    weights, own_weights = [], []
    for n in range(R // STEP):
        requests = range(n * STEP, (n + 1) * STEP)
        heads = [jnp.where(mine_head, qf[r : r + 1, :], 0.0) for r in requests]
        own = [
            jnp.exp(jnp.sum(head * knf[r : r + 1, :], axis=1, keepdims=True) * scale)
            for r, head in zip(requests, heads)
        ]
        keys_in[n].wait()
        scores = [
            lax.dot_general(head.astype(BF), k_s[r], NT, preferred_element_type=F32) * scale
            for r, head in zip(requests, heads)
        ]
        expo = [jnp.where(position < len_s[r], jnp.exp(score), 0.0) for r, score in zip(requests, scores)]
        denom = [jnp.sum(e, axis=1, keepdims=True) + o for e, o in zip(expo, own)]
        weights += [(e / d).astype(BF) for e, d in zip(expo, denom)]
        own_weights += [(o / d).astype(BF).astype(F32) for o, d in zip(own, denom)]
    pl.semaphore_wait(barrier, len(plane) + NZ)
    down_rows = pl.ds(pl.multiple_of(core * 128, 128), 128)
    down_other = pl.ds(pl.multiple_of(other * 128, 128), 128)
    for copy in small[3:]:
        copy.wait()
    vnf[...] = vn_s[...].astype(F32)
    for n in range(R // STEP):
        requests = range(n * STEP, (n + 1) * STEP)
        values_in[n].wait()
        mixed = [
            jnp.dot(weights[r], v_s[r], preferred_element_type=F32) + own_weights[r] * vnf[r : r + 1, :]
            for r in requests
        ]
        for r, part in zip(requests, mixed):
            att[r : r + 1, :] = jnp.sum(jnp.where(mine_head, part, 0.0), axis=0, keepdims=True)
    up_here = fetch(up_ref, wu.at[core], w_loc.at[0])
    send(up_ref, wu.at[core], w_send.at[0], w_recv.at[0], partner)
    values = (resid_s[...].astype(F32) + att[...]).astype(BF).astype(F32)

    def exchange(cb, kb):
        ca, ka = cols - cb, cols - kb
        xa = xbuf.at[:, :, :, 0:ca]
        ya, yr, yl, ra = [ref.at[:, :, 0:ka] for ref in (ya_s, yr_s, yl_s, ra_s)]
        yf, rlr = [ref.at[:, :, :, 0:ka] for ref in (yf_s, rlr_s)]
        ps, qs, rz = [ref.at[:, :, 0:ka] for ref in (ps_s, qs_s, rz_s)]
        tz = tz_s.at[:, 0:ka]
        if cb:
            xb = xb_s.at[:, :, :, 0:cb]
        if kb:
            pb, zs, tb, rxy = pb_s.at[:, :, :, 0:kb], zs_s.at[:, :, :, 0:kb], tb_s.at[:, :, 0:kb], rxy_s.at[:, :, 0:kb]
            zr = zr_s.at[:, :, :, :, 0:kb]

        def slot(i, j):
            return xa.at[(p2 + i) % 4, (p1 + j) % 4]

        def lies(k):
            return pl.ds(DIST.index(k) * R, R)

        gain = jnp.concatenate([gain_s[pl.ds(group(0, 0) * 6 + n, 1), :] for n in range(cols // 128)], axis=1)
        own_mean = jnp.mean(values, axis=1, keepdims=True)
        off = values - own_mean
        scaled = (off * gain).astype(BF)
        mine = slot(0, 0)
        mine[0:R, :] = scaled[:, :ca]
        if cb:
            mine_b = xb.at[0, p2 * 4 + p1]
            mine_b[...] = scaled[:, ca:]

        def copy1(t, c):
            rows = CHUNKS[c]
            send(slot(0, 0).at[rows], slot(0, 0).at[rows], p1_send, p1_recv.at[t - 1, c], near(0, t))

        def copy2(i, j, rows, n, c, to):
            if rows.start < rows.stop:
                sem = p2_recv.at[n, c, j] if n < 2 else p2o_recv.at[j]
                send(slot(i, j).at[rows], slot(i, j).at[rows], p2_send, sem, near(to, 0))

        def spread(j, c):
            copy2(0, j, CHUNKS[c], 0, c, 1)
            copy2(0, j, CHUNKS[c], 1, c, 3)

        def own_part(c):
            for t in (1, 3, 2):
                copy1(t, c)
            spread(0, c)

        def to_z(distances):
            for k in distances:
                send(mine.at[0:R], mine.at[lies(NZ - k)], z_send, z_recv.at[0 if k in (1, 7, 6, 2) else 1], along_z(k))

        to_z((6, 2, 1, 7))
        own_part(0)
        to_z((4, 5, 3))
        for i, j in plane if cb else []:
            send(mine_b, mine_b, xy_send, xy_recv, near(i, j))

        lane = lax.broadcasted_iota(jnp.int32, (R, 128), 1)
        line = lax.broadcasted_iota(jnp.int32, (R, 128), 0)
        g_here = group(0, 0)
        eye = (lane == (g_here % 8) * 16 + line).astype(F32)
        own_sq = jnp.sum(off * off, axis=1, keepdims=True)
        here = stats.at[g_here]
        here[0:1, :] = jnp.sum(own_mean * eye, axis=0, keepdims=True)
        here[1:2, :] = jnp.sum(own_sq * eye, axis=0, keepdims=True)
        for i, j in plane:
            send(here, here, st_send, st_recv, near(i, j))
        down_here = fetch(down_ref, wd.at[down_rows], w_loc.at[1])
        send(down_ref, wd.at[down_rows], w_send.at[1], w_recv.at[1], partner)

        for g in range(16):
            row = jnp.concatenate([gain_s[g * 6 + n : g * 6 + n + 1, :] for n in range(cols // 128)], axis=1)
            high = row.astype(BF).astype(F32)
            upper = lax.broadcasted_iota(jnp.int32, (16, cols), 0) < 8
            gb[g] = jnp.where(upper, high, row - high).astype(BF)

        block0 = z * 32 + group(0, 0)
        hit0 = jnp.max((active_s[...] == block0).astype(F32), axis=1, keepdims=True)
        hit1 = jnp.max((active_s[...] == block0 + 16).astype(F32), axis=1, keepdims=True)
        spans = active_s.shape[0]
        hits = jnp.concatenate([jnp.broadcast_to(hit0, (spans, 128)), jnp.broadcast_to(hit1, (spans, 128))], axis=1)
        row_at = lax.broadcasted_iota(jnp.int32, (ROWS, spans), 0)
        span_at = lax.broadcasted_iota(jnp.int32, (ROWS, spans), 1)
        lie = row_at // R
        away = jnp.where(lie % 2 == 1, (lie + 1) // 2, (NZ - lie // 2) % NZ)
        span_of = (((z + away) % NZ) * 2 + core) * 4 + (row_at % R) // 4
        row_mask = jnp.dot((span_of == span_at).astype(BF), hits.astype(BF), preferred_element_type=F32)
        def by_right(j, c):
            return (slice(0, 16 - 16 * (j % 2)), slice(16, 48), slice(80, 96 + 16 * (j % 2)))[c]

        def by_left(j, c):
            return (slice(16 - 16 * (j % 2), 16), slice(48, 80), slice(96 + 16 * (j % 2), 128))[c]

        def relay1(c):
            for j in (3, 1, 2):
                arrived(slot(0, j).at[CHUNKS[c]], p1_recv.at[3 - j, c])
                spread(j, c)

        def relay2(j, c):
            arrived(slot(3, j).at[CHUNKS[c]], p2_recv.at[0, c, j])
            copy2(3, j, by_right(j, c), 2, c, 1)
            arrived(slot(1, j).at[CHUNKS[c]], p2_recv.at[1, c, j])
            copy2(1, j, by_left(j, c), 3, c, 3)

        def opposite2(j):
            arrived(slot(2, j), p2o_recv.at[j])

        def up(i, j):
            g = group(i, j)
            rows = pl.ds(pl.multiple_of(g * cols, 128), ca)
            both = jnp.concatenate([wu[0, rows, :], wu[1, rows, :]], axis=1)
            if i == 2:
                return jnp.dot(slot(i, j)[...], both, preferred_element_type=F32)
            lines = jnp.concatenate([slot(i, j)[...], gb[g, :, :ca]], axis=0)
            part = jnp.dot(lines, both, preferred_element_type=F32)
            us[g] = part[ROWS:]
            return part[:ROWS]

        def gain_part(i, j):
            g = group(i, j)
            rows = pl.ds(pl.multiple_of(g * cols, 128), ca)
            both = jnp.concatenate([wu[0, rows, :], wu[1, rows, :]], axis=1)
            us[g] = jnp.dot(gb[g, :, :ca], both, preferred_element_type=F32)

        pieces = [slice(0, 8), slice(8, 16)]

        def ring_on(way, step, piece):
            at, to = ((NZ - step) % NZ, NZ - step - 1) if way == 0 else (step, step + 1)
            send(
                xb.at[at, pieces[piece]], xb.at[to, pieces[piece]],
                ring_send, ring_recv.at[way, step, piece], along_z(1 if way == 0 else NZ - 1),
            )

        def ring_in(way, step, piece):
            at = NZ - step if way == 0 else step
            arrived(xb.at[at, pieces[piece]], ring_recv.at[way, step - 1, piece])

        def ring_start():
            if not cb:
                return
            arrived(xb.at[0, 0:15], xy_recv)
            for piece in range(2):
                for way in range(2):
                    ring_on(way, 0, piece)

        def ring_relay(step, piece):
            if not cb:
                return
            for way in range(2):
                ring_in(way, step, piece)
                if step < 3 or piece == way:
                    ring_on(way, step, piece)

        def ring_end():
            ring_in(0, 4, 0)
            ring_in(1, 4, 1)

        def up_b(q2, q1):
            g = (q1 * other + q2 * core) * 4 + q2 * other + q1 * core
            rows = pl.ds(pl.multiple_of(g * cols + ca, 128), cb)
            both = jnp.concatenate([wu[0, rows, :], wu[1, rows, :]], axis=1)
            lines = jnp.concatenate([xb[k, q2 * 4 + q1] for k in DIST] + [gb[g, :, ca:]], axis=0)
            part = jnp.dot(lines, both, preferred_element_type=F32)
            us[g] = us[g] + part[ROWS:]
            return part[:ROWS]

        relay1(0)
        arrived(mine.at[CHUNKS[1]], z_recv.at[0])
        own_part(1)
        ring_start()
        arrived(mine.at[CHUNKS[2]], z_recv.at[1])
        own_part(2)
        relay2(0, 0)
        relay1(1)
        ring_relay(1, 0)
        arrived(stats.at[0:15], st_recv)
        for half in range(2):
            zst[0, 2 * half : 2 * half + 2, :] = jnp.sum(stats[8 * half : 8 * half + 8], axis=0)
        for k in range(1, NZ):
            send(zst.at[0], zst.at[NZ - k], sz_send, sz_recv, along_z(k))
        ring_relay(1, 1)
        relay2(3, 0)
        relay2(1, 0)
        relay2(2, 0)
        relay1(2)
        relay2(0, 1)
        ring_relay(2, 0)
        relay2(3, 1)
        relay2(1, 1)
        ring_relay(2, 1)
        relay2(2, 1)
        relay2(0, 2)
        ring_relay(3, 0)
        relay2(3, 2)
        ring_relay(3, 1)
        relay2(1, 2)
        relay2(2, 2)
        up_here.wait()
        arrived(wu.at[other], w_recv.at[0])
        before = up(0, 0) + up(0, 3)
        before += up(0, 1) + up(0, 2)
        before += up(3, 0) + up(1, 0)
        before += up(3, 3) + up(1, 3)
        before += up(3, 1) + up(1, 1)
        before += up(3, 2) + up(1, 2)

        arrived(zst.at[1:NZ], sz_recv)
        own_lane = lane % 16 == line
        mean_at, square_at = [
            [jnp.concatenate([jnp.where(own_lane, zst[k, 2 * half + n : 2 * half + n + 1, :], 0.0) for k in DIST], axis=0) for half in range(2)]
            for n in range(2)
        ]
        mean_row = jnp.sum(mean_at[0] + mean_at[1], axis=1, keepdims=True) * (1.0 / 16)
        lanes = lax.broadcasted_iota(jnp.int32, (ROWS, 128), 1) % 16 == lax.broadcasted_iota(jnp.int32, (ROWS, 128), 0) % 16
        gaps = [jnp.where(lanes, part - mean_row, 0.0) for part in mean_at]
        var_row = jnp.sum(
            square_at[0] + square_at[1] + cols * (gaps[0] * gaps[0] + gaps[1] * gaps[1]), axis=1, keepdims=True
        ) * (1.0 / width)
        rstd_row = lax.rsqrt(var_row + 1e-05)

        for j in range(4):
            gain_part(2, j)
        if cb:
            ring_end()
        for q in range(16) if cb else []:
            before += up_b(q // 4, q % 4)
        for half in range(2):
            gains = []
            for g in range(8 * half, 8 * half + 8):
                both = us[g, :8, :] + us[g, 8:, :]
                gains += [both, both]
            before += jnp.dot(
                gaps[half], jnp.concatenate(gains, axis=0), preferred_element_type=F32, precision=lax.Precision.HIGHEST
            )
        for j in (0, 3, 1, 2):
            opposite2(j)
            before += up(2, j)
        hidden = (jnp.maximum(before * rstd_row, 0.0) * row_mask).astype(BF)

        down_here.wait()
        arrived(wd.at[down_other], w_recv.at[1])
        back = (2, 3, 1, 0)

        def down(i, j):
            columns = pl.ds(pl.multiple_of(group(i, j) * cols, 128), ka)
            return jnp.dot(hidden, wd[:, columns], preferred_element_type=F32)

        def pass_on(src, dst, j, rows, c, to, s_sem, r_sem):
            if rows.start < rows.stop:
                send(src.at[j, rows], dst.at[j, rows], s_sem, r_sem.at[c, j], near(to, 0))

        def with_arrived(base, j, rows, out):
            if rows.start < rows.stop:
                out[j, rows, :] = (yf[base, j, rows, :] + ra[j, rows, :].astype(F32)).astype(BF)

        def alone(base, j, rows, out):
            if rows.start < rows.stop:
                out[j, rows, :] = yf[base, j, rows, :].astype(BF)

        def start_back(c, slots):
            for j in slots:
                pass_on(ya, ra, j, by_right(j, c), c, 1, a_send, a_recv)
                pass_on(ya, ra, j, by_left(j, c), c, 3, a_send, a_recv)

        def beside_back(j, c):
            alone(0, j, by_left(j, c), yr)
            alone(1, j, by_right(j, c), yl)
            arrived(ra.at[j, CHUNKS[c]], a_recv.at[c, j])
            with_arrived(0, j, by_right(j, c), yr)
            pass_on(yr, rlr.at[0], j, CHUNKS[c], c, 1, b_send.at[0], b_recv)
            with_arrived(1, j, by_left(j, c), yl)
            pass_on(yl, rlr.at[1], j, CHUNKS[c], c, 3, b_send.at[1], b_recv)

        def ring_back(way, k, piece):
            if not kb:
                return
            away = k if way == 0 else NZ - k
            part = pb[away, pieces[piece]]
            if k < 3 or (k == 3 and piece == way):
                arrived(zr.at[way, k, pieces[piece]], back_recv.at[way, k, piece])
                part += zr[way, k, pieces[piece]].astype(F32)
            zs[way * 4 + k - 1, pieces[piece]] = part.astype(BF)
            send(
                zs.at[way * 4 + k - 1, pieces[piece]], zr.at[way, k - 1, pieces[piece]],
                back_send, back_recv.at[way, k - 1, piece], along_z(1 if way == 0 else NZ - 1),
            )

        for j in back:
            ya[j] = down(2, j).astype(BF)
            start_back(2, (j,))
        start_back(0, back)
        start_back(1, back)
        for q2, q1 in [(q // 4, q % 4) for q in range(16)] if kb else []:
            g = (q1 * other + q2 * core) * 4 + q2 * other + q1 * core
            columns = pl.ds(pl.multiple_of(g * cols + ka, 128), kb)
            part = jnp.dot(hidden, wd[:, columns], preferred_element_type=F32)
            for n, k in enumerate(DIST):
                pb[k, q2 * 4 + q1] = part[n * R : (n + 1) * R]
        ring_back(0, 4, 0)
        ring_back(1, 4, 1)
        ring_back(0, 3, 1)
        ring_back(1, 3, 0)
        for j in back:
            yf[0, j] = down(1, j)
            yf[1, j] = down(3, j)
            beside_back(j, 2)
        ring_back(0, 3, 0)
        ring_back(1, 3, 1)
        for j in back:
            beside_back(j, 1)
        ring_back(0, 2, 1)
        ring_back(1, 2, 0)
        for j in back:
            beside_back(j, 0)
        ring_back(0, 2, 0)
        ring_back(1, 2, 1)
        for j in back:
            yf[2, j] = down(0, j)

        def settled(j, c):
            rows = CHUNKS[c]
            arrived(rlr.at[:, j, rows], b_recv.at[c, j])
            return yf[2, j, rows, :] + rlr[0, j, rows, :].astype(F32) + rlr[1, j, rows, :].astype(F32)

        def settle(c):
            rows = CHUNKS[c]
            for j in (2, 3, 1):
                ps[j - 1, rows, :] = settled(j, c).astype(BF)
                send(ps.at[j - 1, rows], qs.at[j - 1, rows], c_send, c_recv.at[c], near(0, j))

        def settle_own(c):
            rows = CHUNKS[c]
            part = settled(0, c)
            arrived(qs.at[:, rows], c_recv.at[c])
            for j in (3, 1, 2):
                part += qs[j - 1, rows, :].astype(F32)
            return part

        def to_owners(c, distances):
            rows = CHUNKS[c]
            tz[rows, :] = settle_own(c).astype(BF)
            for k in distances:
                send(tz.at[lies(k)], rz.at[k - 1], zz_send, zz_recv, along_z(k))

        settle(2)
        ring_back(0, 1, 1)
        ring_back(1, 1, 0)
        settle(1)
        to_owners(2, (4, 3, 5))
        ring_back(0, 1, 0)
        ring_back(1, 1, 1)
        settle(0)
        to_owners(1, (2, 6, 1, 7))
        if kb:
            for piece in range(2):
                for way in range(2):
                    arrived(zr.at[way, 0, pieces[piece]], back_recv.at[way, 0, piece])
            whole = pb[0] + zr[0, 0].astype(F32) + zr[1, 0].astype(F32)
            pb[0] = whole
            tb[...] = whole.astype(BF)
            for n, (i, j) in enumerate(plane):
                send(tb.at[(p2 + i) % 4 * 4 + (p1 + j) % 4], rxy.at[n], xyb_send, xyb_recv, near(i, j))
        total = settle_own(0) + values[:, :ka]
        if kb:
            total_b = pb[0, p2 * 4 + p1] + values[:, ka:]
        arrived(rz, zz_recv)
        for k in range(1, NZ):
            total += rz[k - 1].astype(F32)
        out_ref[:, :ka] = total.astype(BF)
        if kb:
            arrived(rxy, xyb_recv)
            for n in range(len(plane)):
                total_b += rxy[n].astype(F32)
            out_ref[:, ka:] = total_b.astype(BF)
        for src, sem in (
            (up_ref, w_send.at[0]), (down_ref, w_send.at[1]), (stats.at[0:15], st_send), (zst.at[1:NZ], sz_send),
            (mine.at[0 : ROWS - R], z_send), (xa.at[0, 0:3], p1_send), (xa.at[0:3], p2_send), (ya, a_send), (yr, b_send.at[0]), (yl, b_send.at[1]),
            (ps, c_send), (rz, zz_send),
        ):
            sent(src, sem)
        for src, sem in ((xb.at[0, 0:15], xy_send), (xb.at[0:7], ring_send)) if cb else ():
            sent(src, sem)
        for src, sem in ((zs.at[0:7], back_send), (rxy, xyb_send)) if kb else ():
            sent(src, sem)

    for n in range(2):
        pl.when(core == n)(functools.partial(exchange, *CBS[n]))


def layer(resid, query, key_new, value_new, key_cache, value_cache, lengths, norm_gain, active, up, down):
    cols = resid.shape[1]
    width = 16 * cols
    hbm = pl.BlockSpec(memory_space=pl.ANY)
    dma = pltpu.SemaphoreType.DMA
    row = pltpu.VMEM((R, cols), BF)
    row32 = pltpu.VMEM((R, cols), F32)
    cache = pltpu.VMEM((R, 128, cols), BF)
    full = pltpu.VMEM((ROWS, cols), BF)
    four = pltpu.VMEM((4, ROWS, cols), BF)
    ring = (16, R, CB)
    one = dma(())
    return pl.pallas_call(
        layer_kernel,
        out_shape=jax.ShapeDtypeStruct((R, cols), BF),
        in_specs=[hbm] * 11,
        out_specs=pl.BlockSpec(memory_space=pltpu.VMEM),
        scratch_shapes=[
            row, row, row, row, cache, cache,
            pltpu.SMEM((R,), jnp.int32),
            pltpu.VMEM((norm_gain.shape[0] // 128, 128), F32),
            pltpu.VMEM(active.shape, jnp.int32),
            row32, row32, row32, row32,
            pltpu.VMEM((4, 4, ROWS, cols), BF),
            pltpu.VMEM((2, width, 128), BF),
            pltpu.VMEM((256, width), BF),
            pltpu.VMEM((16, 2, 128), F32),
            pltpu.VMEM((16, 16, cols), BF),
            pltpu.VMEM((16, 16, 256), F32),
            pltpu.VMEM((NZ, 4, 128), F32),
            pltpu.VMEM((3, 4, ROWS, cols), F32),
            four, four, four, four,
            pltpu.VMEM((2, 4, ROWS, cols), BF),
            pltpu.VMEM((3, ROWS, cols), BF),
            pltpu.VMEM((3, ROWS, cols), BF),
            full,
            pltpu.VMEM((NZ - 1, R, cols), BF),
            pltpu.VMEM((NZ,) + ring, BF),
            pltpu.VMEM((NZ,) + ring, F32),
            pltpu.VMEM((8,) + ring, BF),
            pltpu.VMEM((2, 4) + ring, BF),
            pltpu.VMEM(ring, BF),
            pltpu.VMEM((15, R, CB), BF),
            dma((7,)), dma((R // STEP,)), dma((R // STEP,)), dma((2,)), dma((2,)), dma((2,)),
            one, one, one, one, one, dma((2,)),
            one, dma((3, 3)), one, dma((2, 3, 4)), dma((4,)),
            one, dma((3, 4)), dma((2,)), dma((3, 4)), one, dma((3,)), one, one,
            one, one, one, dma((2, 4, 2)), one, dma((2, 4, 2)), one, one,
        ],
        compiler_params=pltpu.CompilerParams(
            collective_id=0, has_side_effects=True, vmem_limit_bytes=60 * 1024 * 1024
        ),
        name="layer",
    )(resid, query, key_new, value_new, key_cache, value_cache, lengths, norm_gain.reshape(-1, 128), active, up, down)


def shards(
    resid, query, key_new, value_new, key_cache, value_cache, lengths, norm_gain, active, up_weight, down_weight
):
    return layer(
        resid, query, key_new, value_new, key_cache, value_cache, lengths, norm_gain, active, up_weight, down_weight
    )


def solution(mesh):
    placed = (
        P("attn", ("ffn", "grp")),
        P("attn", ("ffn", "grp")),
        P("attn", ("ffn", "grp")),
        P("attn", ("ffn", "grp")),
        P("attn", None, ("ffn", "grp")),
        P("attn", None, ("ffn", "grp")),
        P("attn"),
        P(),
        P(),
        P(None, ("attn", "ffn", "grp")),
        P(("attn", "ffn", "grp"), None),
    )
    return jax.shard_map(
        shards, mesh=mesh, in_specs=placed, out_specs=P("attn", ("ffn", "grp")), check_vma=False
    )
```
